1024 devices in a mesh: dp: 16 (over x, core), expert: 64 (over y, z).
Axes of the slice: x: 8, y: 8, z: 8, core: 2. Of those that a mesh axis runs over, the one named last changes fastest.
Arguments:
- out_grad: bfloat16 [16384, 7168], P('expert', 'dp'), may hold values from -6 to 6
- inputs: bfloat16 [16384, 7168], P('expert', 'dp'), may hold values from -2.5 to 2.5
- expert_ids: int32 [16384, 8], P('expert'), may hold values from 0 to 255, as said below
- gate_weights: float32 [16384, 8], P('expert'), may hold values from 0.1 to 1
- w_gate: bfloat16 [7168, 32768], P('dp', 'expert'), may hold values from -0.0625 to 0.0625
- w_up: bfloat16 [7168, 32768], P('dp', 'expert'), may hold values from -0.0625 to 0.0625
- w_down: bfloat16 [32768, 7168], P('expert', 'dp'), may hold values from -0.125 to 0.125
Outputs:
- in_grad: bfloat16 [16384, 7168], P('expert', 'dp')
- grad_gate: bfloat16 [7168, 32768], P('dp', 'expert')
- grad_up: bfloat16 [7168, 32768], P('dp', 'expert')
The draws below stay inside these ranges and needn't reach their ends.
Inputs may be any that keep to these rules, and one draw needn't show every extreme that they name: `expert_ids`: each token names 8 different experts. Within one block of 256 consecutive tokens no expert is named by more than 12 tokens, and in every draw some expert below 16 is named by exactly 12 tokens of every block.
All inputs are finite; a program needn't handle non-finite values.
Results may differ from the reference program's by a relative error of at most 0.035.
Values may be sent and summed in bfloat16 or wider, within the bound.
A program may use at most 32 MiB of HBM per device.

```python
import math
import jax
import jax.numpy as jnp
from jax import lax

D = 7168
H = 2048
TOP = 8
ROUTED = 256
TOK_DEV = 256
HSPLIT = 4
CAP = 12
EXPERTS = 16
TOKENS = 16384
N_DP = 16
N_EXPERT = 64


def draw_expert_ids(key, part):
    key = jax.random.fold_in(key, 11)
    scale_unit = TOK_DEV // 128
    leader = jax.random.randint(jax.random.fold_in(key, 1), (), 0, EXPERTS).astype(jnp.int32)
    remaining = jnp.concatenate([jnp.full((7,), 6 * scale_unit, jnp.int32), jnp.full((8,), 4 * scale_unit, jnp.int32), jnp.full((16,), 3 * scale_unit, jnp.int32)])

    def one_block(block_key):
        order_key, count_key, label_key = jax.random.split(block_key, 3)
        shuffled = jax.random.permutation(order_key, ROUTED).astype(jnp.int32)
        position = jnp.argmax(shuffled == leader)
        shuffled = jnp.roll(shuffled, -position)
        counts = jnp.concatenate([jnp.full((1,), 6 * scale_unit, jnp.int32), jax.random.permutation(count_key, remaining)])
        labels = jnp.repeat(jnp.arange(32, dtype=jnp.int32), counts, total_repeat_length=TOK_DEV)
        labels = jax.random.permutation(label_key, labels)
        table_index = labels[:, None] * TOP + jnp.arange(TOP, dtype=jnp.int32)[None, :]
        return shuffled[table_index]
    block_keys = jax.random.split(jax.random.fold_in(key, 2), N_EXPERT)
    return jax.vmap(one_block)(block_keys).reshape(TOKENS, TOP).astype(jnp.int32)


def shard_levels(own_key, extent, cuts, low, top_value):
    def one(dim, blocks):
        steps = jax.random.uniform(jax.random.fold_in(jax.random.fold_in(own_key, 6), dim), (blocks,), jnp.float32, low / len(cuts), top_value / len(cuts))
        return jnp.repeat(jnp.exp(steps), extent[dim] // blocks).reshape((-1,) + (1,) * (len(extent) - dim - 1))

    loudness = one(*cuts[0])
    for cut in cuts[1:]:
        loudness = loudness * one(*cut)
    return loudness


def centred(stream_key, extent, deviation, reach, cuts=(), held_as=jnp.bfloat16):
    array = deviation * jax.random.normal(stream_key, extent, jnp.float32)
    if cuts:
        array = array * shard_levels(stream_key, extent, cuts, -0.22, 0.18)
    return jnp.clip(array, -reach, reach).astype(held_as)


def setup_inputs(seed: int = 0) -> dict:
    key_of = jax.random.split(jax.random.key(seed), 8)
    out_grad = centred(key_of[0], (TOKENS, D), 1.0, 6.0, ((0, 64), (1, 16)))
    inputs = centred(key_of[1], (TOKENS, D), 0.35, 2.5, ((0, 64), (1, 16)))
    expert_ids = draw_expert_ids(jax.random.fold_in(key_of[7], 71), 0)
    gate_weights = jnp.clip(jnp.exp(math.log(1.0) - 2.3025851 * jax.random.uniform(key_of[3], (TOKENS, TOP), jnp.float32) ** shard_levels(key_of[3], (TOKENS, TOP), ((0, 64),), -0.2, 0.2)), 0.1, 1.0)
    w_gate = centred(key_of[4], (D, EXPERTS * H), D ** -0.5, 0.0625, ((0, 16), (1, 64)))
    w_up = centred(key_of[5], (D, EXPERTS * H), D ** -0.5, 0.0625, ((0, 16), (1, 64)))
    w_down = centred(key_of[6], (EXPERTS * H, D), H ** -0.5, 0.125, ((0, 64), (1, 16)))
    return dict(out_grad=out_grad, inputs=inputs, expert_ids=expert_ids, gate_weights=gate_weights, w_gate=w_gate, w_up=w_up, w_down=w_down)


def routes(block_ids, block_gates, experts):
    tokens = block_ids.shape[0]
    flat_ids = block_ids.reshape(-1)
    matches = (flat_ids[:, None] == jnp.arange(experts, dtype=jnp.int32)[None, :]).astype(jnp.int32)
    before = jnp.cumsum(matches, axis=0) - matches
    slot_index = jnp.sum(before * matches, axis=1)
    kept_mask = jnp.sum(matches, axis=1)
    target = jnp.where(kept_mask > 0, flat_ids * CAP + slot_index, -1)
    columns = jnp.arange(experts * CAP, dtype=jnp.int32)
    onehot = (target[:, None] == columns[None, :]).astype(jnp.float32)
    weighted = onehot * block_gates.reshape(-1)[:, None]
    chosen = jnp.sum(onehot.reshape(tokens, TOP, -1), axis=1)
    scaled = jnp.sum(weighted.reshape(tokens, TOP, -1), axis=1)
    return chosen, scaled


def block_sum(left, right):
    parts = jnp.einsum('rjd,jdh->jrh', left, right)
    rounded = lax.optimization_barrier(parts.astype(jnp.bfloat16))
    return jnp.sum(rounded.astype(jnp.float32), axis=0)


def expert_backward(operands):
    grad_rows, input_rows, gate_cols, up_cols, down_rows = operands
    row_count = grad_rows.shape[0]
    feature_block = D // N_DP
    quarter_width = H // HSPLIT
    grad_split = grad_rows.astype(jnp.float32).reshape(row_count, N_DP, feature_block)
    input_split = input_rows.astype(jnp.float32).reshape(row_count, N_DP, feature_block)
    down_split = down_rows.astype(jnp.float32).reshape(H, N_DP, feature_block).transpose(1, 2, 0)
    hidden_grad = block_sum(grad_split, down_split)
    gate_pre = block_sum(input_split, gate_cols.astype(jnp.float32).reshape(N_DP, feature_block, H))
    up_pre = block_sum(input_split, up_cols.astype(jnp.float32).reshape(N_DP, feature_block, H))
    sigma = jax.nn.sigmoid(gate_pre)
    grad_gate_pre = (hidden_grad * up_pre * sigma * (1.0 + gate_pre * (1.0 - sigma))).astype(jnp.bfloat16)
    grad_up_pre = (hidden_grad * gate_pre * sigma).astype(jnp.bfloat16)
    gate_q = grad_gate_pre.astype(jnp.float32).reshape(row_count, HSPLIT, quarter_width)
    up_q = grad_up_pre.astype(jnp.float32).reshape(row_count, HSPLIT, quarter_width)
    quarters = jnp.einsum('rqh,dqh->qrd', gate_q, gate_cols.astype(jnp.float32).reshape(D, HSPLIT, quarter_width))
    quarters = quarters + jnp.einsum('rqh,dqh->qrd', up_q, up_cols.astype(jnp.float32).reshape(D, HSPLIT, quarter_width))
    rounded = lax.optimization_barrier(quarters.astype(jnp.bfloat16))
    returned = jnp.sum(rounded.astype(jnp.float32), axis=0)
    grad_gate = jnp.dot(input_rows.T, grad_gate_pre, preferred_element_type=jnp.float32).astype(jnp.bfloat16)
    grad_up = jnp.dot(input_rows.T, grad_up_pre, preferred_element_type=jnp.float32).astype(jnp.bfloat16)
    return returned, grad_gate, grad_up


def reference(out_grad, inputs, expert_ids, gate_weights, w_gate, w_up, w_down):
    blocks = N_EXPERT
    experts = EXPERTS
    row_count = blocks * CAP
    routed_ids = expert_ids.reshape(blocks, TOK_DEV, TOP)
    gate_blocks = gate_weights.reshape(blocks, TOK_DEV, TOP)
    chosen, scaled = jax.vmap(lambda a, b: routes(a, b, experts))(routed_ids, gate_blocks)
    grad_rows = out_grad.astype(jnp.float32).reshape(blocks, TOK_DEV, D)
    input_rows = inputs.astype(jnp.float32).reshape(blocks, TOK_DEV, D)
    sent_grad = jnp.einsum('btr,btd->rbd', scaled, grad_rows, precision=lax.Precision.HIGHEST).astype(jnp.bfloat16)
    sent_input = jnp.einsum('btr,btd->rbd', chosen, input_rows, precision=lax.Precision.HIGHEST).astype(jnp.bfloat16)
    sent_grad = sent_grad.reshape(experts, CAP, blocks, D).transpose(0, 2, 1, 3).reshape(experts, row_count, D)
    sent_input = sent_input.reshape(experts, CAP, blocks, D).transpose(0, 2, 1, 3).reshape(experts, row_count, D)
    gate_cols = w_gate.reshape(D, experts, H).transpose(1, 0, 2)
    up_cols = w_up.reshape(D, experts, H).transpose(1, 0, 2)
    down_rows = w_down.reshape(experts, H, D)
    returned, grad_gate, grad_up = lax.map(expert_backward, (sent_grad, sent_input, gate_cols, up_cols, down_rows))
    returned = returned.reshape(experts, blocks, CAP, D).transpose(1, 0, 2, 3).reshape(blocks, experts * CAP, D)
    in_grad = jnp.einsum('btr,brd->btd', chosen, returned, precision=lax.Precision.HIGHEST)
    in_grad = in_grad.reshape(TOKENS, D).astype(jnp.bfloat16)
    grad_gate = grad_gate.transpose(1, 0, 2).reshape(D, experts * H)
    grad_up = grad_up.transpose(1, 0, 2).reshape(D, experts * H)
    return in_grad, grad_gate, grad_up
```

```python
import functools

import jax
import jax.numpy as jnp
from jax import lax
from jax.experimental import pallas as pl
from jax.experimental.pallas import tpu as pltpu
from jax.sharding import PartitionSpec as P

HSPLIT = 4
CAP = 12
SLOT = 16
CORES = 2
BF = jnp.bfloat16
F32 = jnp.float32


def grid_of(devices):
    side = 1
    while side * side < devices:
        side *= 2
    return devices // side, side


def mm(a, b):
    return lax.dot_general(a, b, (((1,), (0,)), ((), ())), preferred_element_type=F32)


def mm_nt(a, b):
    return lax.dot_general(a, b, (((1,), (1,)), ((), ())), preferred_element_type=F32)


def mm_tn(a, b):
    return lax.dot_general(a, b, (((0,), (0,)), ((), ())), preferred_element_type=F32)


def iota(shape, dim):
    return lax.broadcasted_iota(jnp.int32, shape, dim)


def near_first(n):
    order = []
    for k in range(1, n // 2 + 1):
        order.append(k)
        if n - k != k:
            order.append(n - k)
    return order


def kernel(
    sizes,
    out_grad,
    inputs,
    ids,
    gates,
    w_gate,
    w_up,
    w_down,
    in_grad,
    grad_gate,
    grad_up,
    picker_t,
    ysend,
    yrecv,
    zsend,
    rows,
    csend,
    crecv,
    own,
    rsend,
    rrecv,
    acts,
    back,
    zret,
    yback,
    yret,
    y_ss,
    y_rs,
    z_ss,
    z_rs,
    c_ss,
    c_rs,
    r_ss,
    r_rs,
    a_ss,
    a_rs,
    s_ss,
    s_rs,
    b_ss,
    b_rs,
    e_ss,
    e_rs,
):
    nx, ny, nz = sizes
    groups = nz // HSPLIT
    blk = groups * SLOT
    slots = ny * blk
    per_z = ny * CAP
    tokens = out_grad.shape[0]
    half = w_gate.shape[1] // CORES

    dp = lax.axis_index("dp")
    ex = lax.axis_index("expert")
    x, core = dp // CORES, dp % CORES
    y, z = ex // nz, ex % nz
    zgroup = z // HSPLIT
    sibling = (x * CORES + 1 - core, ex)

    def at_y(k):
        t = (y + k) % ny
        return t, (dp, t * nz + z)

    def at_z(k):
        t = (z + k) % nz
        return t, (dp, y * nz + t)

    def at_x(k):
        t = (x + k) % nx
        return t, (t * CORES + core, ex)

    def remote(src, dst, ssem, rsem, device):
        return pltpu.make_async_remote_copy(
            src_ref=src,
            dst_ref=dst,
            send_sem=ssem,
            recv_sem=rsem,
            device_id=device,
            device_id_type=pl.DeviceIdType.MESH,
        )

    partners = (
        [at_y(k)[1] for k in range(1, ny)]
        + [at_z(k)[1] for k in range(1, nz)]
        + [at_x(k)[1] for k in range(1, nx)]
        + [sibling]
    )
    barrier = pltpu.get_barrier_semaphore()
    for device in partners:
        pl.semaphore_signal(barrier, inc=1, device_id=device, device_id_type=pl.DeviceIdType.MESH)

    lane = iota((tokens, 128), 1)
    hits = jnp.zeros((tokens, 128), F32)
    gate = jnp.zeros((tokens, 128), F32)
    for k in range(ids.shape[1]):
        hit = ids[:, k : k + 1] == lane
        hits = hits + jnp.where(hit, 1.0, 0.0)
        gate = gate + jnp.where(hit, gates[:, k : k + 1], 0.0)
    hits_b = hits.astype(BF)
    before = jnp.where(iota((tokens, tokens), 0) > iota((tokens, tokens), 1), 1.0, 0.0).astype(BF)
    slot_of = mm(before, hits_b).astype(BF)
    expand = jnp.where(iota((slots, 128), 0) // SLOT == iota((slots, 128), 1), 1.0, 0.0).astype(BF)
    hit_rt = mm_nt(expand, hits_b)
    slot_rt = mm_nt(expand, slot_of)
    wanted = (iota((slots, tokens), 0) % SLOT).astype(F32)
    picker = jnp.where(jnp.logical_and(hit_rt > 0.5, slot_rt == wanted), 1.0, 0.0)
    gate_1 = gate.astype(BF)
    rest = gate - gate_1.astype(F32)
    gate_2 = rest.astype(BF)
    gate_3 = (rest - gate_2.astype(F32)).astype(BF)
    gate_rt = mm_nt(expand, gate_1) + mm_nt(expand, gate_2) + mm_nt(expand, gate_3)
    scale = jnp.sum(picker * gate_rt, axis=1, keepdims=True)
    picker_b = picker.astype(BF)
    hit_tr = mm_nt(hits_b, expand)
    slot_tr = mm_nt(slot_of, expand)
    wanted_t = (iota((tokens, slots), 1) % SLOT).astype(F32)
    picker_t[...] = jnp.where(
        jnp.logical_and(hit_tr > 0.5, slot_tr == wanted_t), 1.0, 0.0
    ).astype(BF)

    def block(ref, index, count, *lead):
        return ref.at[(*lead, pl.ds(pl.multiple_of(index * count, 16), count))]

    def y_copies(a, source, target, ss, rs):
        copies = {}
        for k in near_first(ny):
            t, device = at_y(k)
            copies[k] = remote(
                block(source, t, blk, a),
                block(target, y, blk, a),
                ss.at[a, k],
                rs.at[a, k],
                device,
            )
        return copies

    ysend[0] = mm(picker_b, inputs[...]).astype(BF)
    pl.semaphore_wait(barrier, len(partners))
    y_in = y_copies(0, ysend, yrecv, y_ss, y_rs)
    for copy in y_in.values():
        copy.start()
    ysend[1] = (scale * mm(picker_b, out_grad[...])).astype(BF)
    y_gr = y_copies(1, ysend, yrecv, y_ss, y_rs)
    for copy in y_gr.values():
        copy.start()

    col = iota((groups * per_z, slots), 1)
    seat = (col // SLOT % groups) * per_z + (col // blk) * CAP + col % SLOT
    pack = jnp.where(
        jnp.logical_and(seat == iota((groups * per_z, slots), 0), col % SLOT < CAP), 1.0, 0.0
    ).astype(BF)
    row = iota((slots, groups * per_z), 0)
    seat_t = (row // SLOT % groups) * per_z + (row // blk) * CAP + row % SLOT
    unpack = jnp.where(
        jnp.logical_and(seat_t == iota((slots, groups * per_z), 1), row % SLOT < CAP), 1.0, 0.0
    ).astype(BF)

    def z_phase(a, y_in_flight):
        here = pl.ds(pl.multiple_of(y * blk, 16), blk)
        yrecv[a, here] = ysend[a, here]
        for copy in y_in_flight.values():
            copy.wait_recv()
        zsend[a] = mm(pack, yrecv[a]).astype(BF)
        copies = {}
        for k in near_first(nz):
            t, device = at_z(k)
            copies[k] = remote(
                block(zsend, t // HSPLIT, per_z, a),
                block(rows, z, per_z, a),
                z_ss.at[a, k],
                z_rs.at[a, k],
                device,
            )
            copies[k].start()
        rows[a, pl.ds(pl.multiple_of(z * per_z, 16), per_z)] = zsend[
            a, pl.ds(pl.multiple_of(zgroup * per_z, 16), per_z)
        ]
        return copies

    total = nz * per_z
    chunk = total // 2

    def product(a, w, out, mine, transposed):
        which = core if mine else 1 - core
        start = pl.multiple_of(which * half, 128)

        def body(i, _):
            at = pl.ds(pl.multiple_of(i * chunk, 16), chunk)
            left = rows[a, at]
            if transposed:
                value = mm_nt(left, w[pl.ds(start, half), :])
            else:
                value = mm(left, w[:, pl.ds(start, half)])
            out[at] = value.astype(out.dtype)
            return 0

        lax.fori_loop(0, 2, body, 0)

    def cores_start(n):
        copy = remote(csend.at[n], crecv.at[n], c_ss.at[n], c_rs.at[n], sibling)
        copy.start()
        return copy

    shard = total // nx

    def x_scatter(n, core_copy):
        core_copy.wait_recv()

        def body(i, _):
            at = pl.ds(pl.multiple_of(i * shard, 16), shard)
            value = own[n, at] + crecv[n, at].astype(F32)
            own[n, at] = value
            rsend[n, at] = value.astype(BF)
            return 0

        lax.fori_loop(0, nx, body, 0)
        copies = {}
        for k in near_first(nx):
            t, device = at_x(k)
            copies[k] = remote(
                block(rsend, t, shard, n),
                block(rrecv, x, shard, n),
                r_ss.at[n, k],
                r_rs.at[n, k],
                device,
            )
            copies[k].start()
        return copies

    z_in = z_phase(0, y_in)
    for copy in z_in.values():
        copy.wait_recv()
    z_gr = z_phase(1, y_gr)

    product(0, w_gate, csend.at[0], False, False)
    c_gate = cores_start(0)
    product(0, w_up, csend.at[1], False, False)
    c_up = cores_start(1)
    product(0, w_gate, own.at[0], True, False)
    r_gate = x_scatter(0, c_gate)
    product(0, w_up, own.at[1], True, False)
    r_up = x_scatter(1, c_up)

    for copy in z_gr.values():
        copy.wait_recv()
    product(1, w_down, csend.at[2], False, True)
    c_down = cores_start(2)
    product(1, w_down, own.at[2], True, True)
    r_down = x_scatter(2, c_down)

    mine = pl.ds(pl.multiple_of(x * shard, 16), shard)

    def x_sum(n, copies):
        value = own[n, mine]
        for k in copies:
            copies[k].wait_recv()
        for k in copies:
            source = (x + nx - k) % nx
            value = value + rrecv[n, pl.ds(pl.multiple_of(source * shard, 16), shard)].astype(F32)
        return value

    gate_pre = x_sum(0, r_gate)
    up_pre = x_sum(1, r_up)
    sigma = 1.0 / (1.0 + jnp.exp(-gate_pre))
    gate_factor = up_pre * sigma * (1.0 + gate_pre * (1.0 - sigma))
    up_factor = gate_pre * sigma
    hidden_grad = x_sum(2, r_down)
    acts[core, mine] = (hidden_grad * gate_factor).astype(BF)
    acts[CORES + core, mine] = (hidden_grad * up_factor).astype(BF)

    def to_sibling(a, k):
        source = (x + nx - k) % nx
        view = block(acts, source, shard, a * CORES + core)
        return remote(view, view, s_ss.at[a, k], s_rs.at[a, k], sibling)

    gathers = []
    for k in near_first(nx):
        for a in range(2):
            _, device = at_x(k)
            view = block(acts, x, shard, a * CORES + core)
            copy = remote(view, view, a_ss.at[a, k], a_rs.at[a, k], device)
            copy.start()
            gathers.append((a, k, copy))
    forwards = []
    for a in range(2):
        copy = to_sibling(a, 0)
        copy.start()
        forwards.append(copy)
    for a, k, copy in gathers:
        copy.wait_recv()
        copy = to_sibling(a, k)
        copy.start()
        forwards.append(copy)
    for copy in forwards:
        copy.wait_recv()

    def back_body(i, _):
        at = pl.ds(pl.multiple_of(i * chunk, 16), chunk)
        value = None
        for a, w in ((0, w_gate), (1, w_up)):
            for c in range(CORES):
                term = mm_nt(acts[a * CORES + c, at], w[:, c * half : (c + 1) * half])
                value = term if value is None else value + term
        back[at] = value.astype(BF)
        return 0

    lax.fori_loop(0, 2, back_body, 0)

    z_back = {}
    for k in near_first(nz):
        t, device = at_z(k)
        z_back[k] = remote(
            block(back, t, per_z), block(zret, z, per_z), b_ss.at[k], b_rs.at[k], device
        )
        z_back[k].start()
    at_mine = pl.ds(pl.multiple_of(z * per_z, 16), per_z)
    zret[at_mine] = back[at_mine]

    for a, grad in ((0, grad_gate), (1, grad_up)):
        for c in range(CORES):
            grad[:, c * half : (c + 1) * half] = mm_tn(rows[0], acts[a * CORES + c]).astype(BF)

    for copy in z_back.values():
        copy.wait_recv()
    sums = []
    for g in range(groups):
        value = None
        for q in range(HSPLIT):
            first = (g * HSPLIT + q) * per_z
            term = zret[first : first + per_z].astype(F32)
            value = term if value is None else value + term
        sums.append(value.astype(BF))
    spread = None
    for g in range(groups):
        term = mm(unpack[:, g * per_z : (g + 1) * per_z], sums[g])
        spread = term if spread is None else spread + term
    yback[...] = spread.astype(BF)
    y_back = {}
    for k in near_first(ny):
        t, device = at_y(k)
        y_back[k] = remote(block(yback, t, blk), block(yret, y, blk), e_ss.at[k], e_rs.at[k], device)
        y_back[k].start()
    here = pl.ds(pl.multiple_of(y * blk, 16), blk)
    yret[here] = yback[here]
    for copy in y_back.values():
        copy.wait_recv()
    in_grad[...] = mm(picker_t[...], yret[...]).astype(BF)

    for copies in (y_in, y_gr, z_in, z_gr, r_gate, r_up, r_down, z_back, y_back):
        for copy in copies.values():
            copy.wait_send()
    for copy in (c_gate, c_up, c_down):
        copy.wait_send()
    for _, _, copy in gathers:
        copy.wait_send()
    for copy in forwards:
        copy.wait_send()


def per_device(sizes, out_grad, inputs, expert_ids, gate_weights, w_gate, w_up, w_down):
    nx, ny, nz = sizes
    tokens, feature = out_grad.shape
    hidden = w_gate.shape[1]
    half = hidden // CORES
    groups = nz // HSPLIT
    slots = ny * groups * SLOT
    per_z = ny * CAP
    total = nz * per_z
    dma = pltpu.SemaphoreType.DMA
    vmem = pltpu.VMEM
    return pl.pallas_call(
        functools.partial(kernel, sizes),
        out_shape=(
            jax.ShapeDtypeStruct((tokens, feature), BF),
            jax.ShapeDtypeStruct((feature, hidden), BF),
            jax.ShapeDtypeStruct((feature, hidden), BF),
        ),
        in_specs=[pl.BlockSpec(memory_space=vmem)] * 7,
        out_specs=(pl.BlockSpec(memory_space=vmem),) * 3,
        scratch_shapes=[
            vmem((tokens, slots), BF),
            vmem((2, slots, feature), BF),
            vmem((2, slots, feature), BF),
            vmem((2, groups * per_z, feature), BF),
            vmem((2, total, feature), BF),
            vmem((3, total, half), BF),
            vmem((3, total, half), BF),
            vmem((3, total, half), F32),
            vmem((3, total, half), BF),
            vmem((3, total, half), BF),
            vmem((2 * CORES, total, half), BF),
            vmem((total, feature), BF),
            vmem((total, feature), BF),
            vmem((slots, feature), BF),
            vmem((slots, feature), BF),
            dma((2, ny)),
            dma((2, ny)),
            dma((2, nz)),
            dma((2, nz)),
            dma((3,)),
            dma((3,)),
            dma((3, nx)),
            dma((3, nx)),
            dma((2, nx)),
            dma((2, nx)),
            dma((2, nx)),
            dma((2, nx)),
            dma((nz,)),
            dma((nz,)),
            dma((ny,)),
            dma((ny,)),
        ],
        compiler_params=pltpu.CompilerParams(
            collective_id=0, has_side_effects=True, vmem_limit_bytes=48 * 1024 * 1024
        ),
        cost_estimate=pl.CostEstimate(
            flops=14 * total * feature * hidden, bytes_accessed=4_000_000, transcendentals=0
        ),
    )(out_grad, inputs, expert_ids, gate_weights, w_gate, w_up, w_down)


def solution(mesh, sizes=None):
    if sizes is None:
        ny, nz = grid_of(mesh.shape["expert"])
        sizes = (mesh.shape["dp"] // CORES, ny, nz)
    placed = (
        P("expert", "dp"),
        P("expert", "dp"),
        P("expert", None),
        P("expert", None),
        P("dp", "expert"),
        P("dp", "expert"),
        P("expert", "dp"),
    )
    return jax.shard_map(
        functools.partial(per_device, sizes),
        mesh=mesh,
        in_specs=placed,
        out_specs=(P("expert", "dp"), P("dp", "expert"), P("dp", "expert")),
        check_vma=False,
    )
```

```python
import functools

import jax
import jax.numpy as jnp
from jax import lax
from jax.experimental import pallas as pl
from jax.experimental.pallas import tpu as pltpu
from jax.sharding import PartitionSpec as P

HSPLIT = 4
CAP = 12
SLOT = 16
PARTS = (48, 48)
CHUNKS = len(PARTS)
Z_FIRST = (
    ((0, 1), (1, 1), (1, 3)),
    ((0, 2), (1, 3), (1, 0), (0, 0)),
    ((0, 1), (1, 0), (1, 3), (0, 3)),
    ((0, 2), (1, 2), (1, 0)),
)
Z_SECOND = (
    ((7, 1), (6, 1), (5, 1)),
    ((0, 3), (0, 2), (4, 0), (2, 0)),
    ((3, 0), (3, 1), (7, 3), (1, 3)),
    ((4, 2), (5, 2), (6, 2)),
)
CORES = 2
BF = jnp.bfloat16
F32 = jnp.float32


def grid_of(devices):
    side = 1
    while side * side < devices:
        side *= 2
    return devices // side, side


def mm(a, b):
    return lax.dot_general(a, b, (((1,), (0,)), ((), ())), preferred_element_type=F32)


def mm_nt(a, b):
    return lax.dot_general(a, b, (((1,), (1,)), ((), ())), preferred_element_type=F32)


def mm_tn(a, b):
    return lax.dot_general(a, b, (((0,), (0,)), ((), ())), preferred_element_type=F32)


def iota(shape, dim):
    return lax.broadcasted_iota(jnp.int32, shape, dim)


def near_first(n):
    order = []
    for k in range(1, n // 2 + 1):
        order.append(k)
        if n - k != k:
            order.append(n - k)
    return order


def kernel(
    sizes,
    out_grad_t,
    inputs_t,
    ids_t,
    gates_t,
    w_gate,
    w_up,
    w_down_t,
    in_grad_t,
    grad_gate,
    grad_up,
    pick,
    ysend,
    yrecv,
    zsend,
    rows,
    csend,
    crecv,
    own,
    rsend,
    rrecv,
    xcomb,
    acts,
    back,
    zret,
    yback,
    yret,
    y_ss,
    y_rs,
    z_ss,
    z_rs,
    c_ss,
    c_rs,
    r_ss,
    r_rs,
    a_ss,
    a_rs,
    s_ss,
    s_rs,
    b_ss,
    b_rs,
    e_ss,
    e_rs,
):
    nx, ny, nz = sizes
    groups = nz // HSPLIT
    blk = groups * SLOT
    slots = ny * blk
    per_z = ny * CAP
    tokens = ids_t.shape[1]
    half = w_gate.shape[1] // CORES

    dp = lax.axis_index("dp")
    ex = lax.axis_index("expert")
    x, core = dp // CORES, dp % CORES
    y, z = ex // nz, ex % nz
    zgroup = z // HSPLIT
    sibling = (x * CORES + 1 - core, ex)

    def at_y(k):
        t = (y + k) % ny
        return t, (dp, t * nz + z)

    def at_z(k):
        t = (z + k) % nz
        return t, (dp, y * nz + t)

    def at_x(k):
        t = (x + k) % nx
        return t, (t * CORES + core, ex)

    def remote(src, dst, ssem, rsem, device):
        return pltpu.make_async_remote_copy(
            src_ref=src,
            dst_ref=dst,
            send_sem=ssem,
            recv_sem=rsem,
            device_id=device,
            device_id_type=pl.DeviceIdType.MESH,
        )

    partners = (
        [at_y(k)[1] for k in range(1, ny)]
        + [at_z(k)[1] for k in range(1, nz)]
        + [at_x(k)[1] for k in range(1, nx)]
        + [sibling]
    )
    barrier = pltpu.get_barrier_semaphore()
    for device in partners:
        pl.semaphore_signal(barrier, inc=1, device_id=device, device_id_type=pl.DeviceIdType.MESH)

    expert = iota((128, tokens), 0)
    hits = jnp.zeros((128, tokens), F32)
    gate = jnp.zeros((128, tokens), F32)
    for k in range(ids_t.shape[0]):
        hit = ids_t[k : k + 1, :] == expert
        hits = hits + jnp.where(hit, 1.0, 0.0)
        gate = gate + jnp.where(hit, gates_t[k : k + 1, :], 0.0)
    hits_b = hits.astype(BF)
    before = jnp.where(iota((tokens, tokens), 0) < iota((tokens, tokens), 1), 1.0, 0.0).astype(BF)
    slot_of = mm(hits_b, before).astype(BF)
    expand = jnp.where(iota((slots, 128), 0) // SLOT == iota((slots, 128), 1), 1.0, 0.0).astype(BF)
    hit_rt = mm(expand, hits_b)
    slot_rt = mm(expand, slot_of)
    wanted = (iota((slots, tokens), 0) % SLOT).astype(F32)
    picker = jnp.where(jnp.logical_and(hit_rt > 0.5, slot_rt == wanted), 1.0, 0.0)
    picker_b = picker.astype(BF)
    pick[...] = picker_b

    def block(ref, index, count, *lead):
        return ref.at[(*lead, pl.ds(pl.multiple_of(index * count, 16), count))]

    def y_copies(a):
        copies = {}
        for k in near_first(ny):
            t, device = at_y(k)
            copies[k] = remote(
                block(ysend, t, blk, a),
                block(yrecv, y, blk, a),
                y_ss.at[a, k],
                y_rs.at[a, k],
                device,
            )
            copies[k].start()
        return copies

    ysend[0] = mm_nt(picker_b, inputs_t[...]).astype(BF)
    pl.semaphore_wait(barrier, len(partners))
    y_in = y_copies(0)
    gate_1 = gate.astype(BF)
    rest = gate - gate_1.astype(F32)
    gate_2 = rest.astype(BF)
    gate_3 = (rest - gate_2.astype(F32)).astype(BF)
    gate_rt = mm(expand, gate_1) + mm(expand, gate_2) + mm(expand, gate_3)
    scale = jnp.sum(picker * gate_rt, axis=1, keepdims=True)
    ysend[1] = (scale * mm_nt(picker_b, out_grad_t[...])).astype(BF)
    y_gr = y_copies(1)

    col = iota((groups * per_z, slots), 1)
    seat = (col // SLOT % groups) * per_z + (col // blk) * CAP + col % SLOT
    pack = jnp.where(
        jnp.logical_and(seat == iota((groups * per_z, slots), 0), col % SLOT < CAP), 1.0, 0.0
    ).astype(BF)
    row = iota((slots, groups * per_z), 0)
    seat_t = (row // SLOT % groups) * per_z + (row // blk) * CAP + row % SLOT
    unpack = jnp.where(
        jnp.logical_and(seat_t == iota((slots, groups * per_z), 1), row % SLOT < CAP), 1.0, 0.0
    ).astype(BF)

    def arrived(copies):
        for copy in copies.values():
            copy.wait_recv()

    def pack_rows(a, y_in_flight):
        here = pl.ds(pl.multiple_of(y * blk, 16), blk)
        yrecv[a, here] = ysend[a, here]
        arrived(y_in_flight)
        packed = mm(pack, yrecv[a]).astype(BF)
        for g in range(groups):
            for ch in range(CHUNKS):
                first = g * per_z + starts[ch]
                zsend[(a * CHUNKS + ch) * groups + g, : PARTS[ch]] = packed[
                    first : first + PARTS[ch]
                ]

    place = z % HSPLIT

    def z_device(other, to):
        group = 1 - zgroup if other else zgroup
        return (dp, y * nz + group * HSPLIT + to)

    def z_rows(n, ch, source):
        return block(rows, source, PARTS[ch], n)

    def z_source(tag):
        group = 1 - zgroup if tag >= HSPLIT else zgroup
        return group * HSPLIT + tag % HSPLIT

    def z_first(n, ch, at, j):
        other, to = Z_FIRST[at][j]
        group = 1 - zgroup if other else zgroup
        tag = at + HSPLIT * other
        return remote(
            zsend.at[n * groups + group, pl.ds(0, PARTS[ch])],
            z_rows(n, ch, z),
            z_ss.at[n, j],
            z_rs.at[n, tag],
            z_device(other, to),
        )

    def z_second(n, ch, at, j):
        tag, to = Z_SECOND[at][j]
        view = z_rows(n, ch, z_source(tag))
        return remote(view, view, z_ss.at[n, 4 + j], z_rs.at[n, tag], z_device(False, to))

    def z_arrival(n, ch, tag):
        view = z_rows(n, ch, z_source(tag))
        remote(view, view, z_ss.at[n, 0], z_rs.at[n, tag], sibling).wait_recv()

    def each_place(step):
        for at in range(HSPLIT):
            pl.when(place == at)(functools.partial(step, at))

    def z_start(a, ch):
        n = a * CHUNKS + ch
        part = PARTS[ch]

        def step(at):
            for j in range(len(Z_FIRST[at])):
                z_first(n, ch, at, j).start()

        each_place(step)
        rows[n, pl.ds(pl.multiple_of(z * part, 16), part)] = zsend[n * groups + zgroup, :part]

    def z_pass(a, ch):
        n = a * CHUNKS + ch

        def step(at):
            done = []
            for j, (tag, _) in enumerate(Z_SECOND[at]):
                if tag not in done:
                    z_arrival(n, ch, tag)
                    done.append(tag)
                z_second(n, ch, at, j).start()

        each_place(step)

    def z_finish(a, ch):
        n = a * CHUNKS + ch

        def step(at):
            passed = [tag for tag, _ in Z_SECOND[at]]
            for tag in range(nz):
                if tag != at and tag not in passed:
                    z_arrival(n, ch, tag)

        each_place(step)

    def z_sent(n, ch):
        def step(at):
            for j in range(len(Z_FIRST[at])):
                z_first(n, ch, at, j).wait_send()
            for j in range(len(Z_SECOND[at])):
                z_second(n, ch, at, j).wait_send()

        each_place(step)

    def product(a, ch, w, mine):
        start = pl.multiple_of((core if mine else 1 - core) * half, 128)
        return mm(rows[a * CHUNKS + ch, : nz * PARTS[ch]], w[:, pl.ds(start, half)])

    def cores_send(p, ch, a, w):
        n = p * CHUNKS + ch
        total = nz * PARTS[ch]
        csend[n, :total] = product(a, ch, w, False).astype(BF)
        at = pl.ds(0, total)
        copy = remote(csend.at[n, at], crecv.at[n, at], c_ss.at[n], c_rs.at[n], sibling)
        copy.start()
        return copy

    def shard_at(ch, k):
        shard = nz * PARTS[ch] // nx
        return pl.ds(pl.multiple_of((x + nx + k) % nx * shard, 16), shard)

    def x_copy(n, ch, role, source, k):
        where = pl.ds(0, nz * PARTS[ch] // nx)
        return remote(
            source, rrecv.at[n, role, where], r_ss.at[n, role], r_rs.at[n, role], at_x(k + nx)[1]
        )

    def x_scatter(p, ch, a, w, core_copy):
        n = p * CHUNKS + ch
        total = nz * PARTS[ch]
        value = product(a, ch, w, True)
        core_copy.wait_recv()
        value = value + crecv[n, :total].astype(F32)
        own[n, :total] = value
        rsend[n, :total] = value.astype(BF)
        copies = {}
        if nx > 1:
            far = 2 if (p + ch) % 2 == 0 else -2
            for role, shard, k in ((4, 4, far), (2, 3, 1), (3, -3, -1), (0, 1, 1), (1, -1, -1)):
                copies[role] = x_copy(n, ch, role, rsend.at[n, shard_at(ch, shard)], k)
                copies[role].start()
        return copies

    def x_combine(p, ch, copies):
        n = p * CHUNKS + ch
        shard = nz * PARTS[ch] // nx
        if nx > 1:
            even = (p + ch) % 2 == 0
            copies[2].wait_recv()
            copies[3].wait_recv()
            copies[4].wait_recv()
            for i, k in ((0, 2), (1, -2)) if even else ((1, -2), (0, 2)):
                value = own[n, shard_at(ch, k)] + rrecv[n, 2 + i, :shard].astype(F32)
                if even == (i == 0):
                    value = value + rrecv[n, 4, :shard].astype(F32)
                xcomb[n, i, :shard] = value.astype(BF)
                copies[5 + i] = x_copy(n, ch, 5 + i, xcomb.at[n, i, pl.ds(0, shard)], k)
                copies[5 + i].start()

    def x_sum(p, ch, copies):
        n = p * CHUNKS + ch
        shard = nz * PARTS[ch] // nx
        value = own[n, shard_at(ch, 0)]
        for role in (0, 1, 5, 6) if nx > 1 else ():
            copies[role].wait_recv()
            value = value + rrecv[n, role, :shard].astype(F32)
        return value

    def act_view(a, ch, k):
        return acts.at[(a * CHUNKS + ch) * CORES + core, shard_at(ch, k)]

    def to_sibling(a, ch, k):
        n = a * CHUNKS + ch
        view = act_view(a, ch, -k)
        copy = remote(view, view, s_ss.at[n, k], s_rs.at[n, k], sibling)
        copy.start()
        return copy

    def gather_copy(a, ch, k, away, target):
        n = a * CHUNKS + ch
        view = act_view(a, ch, away)
        return remote(view, view, a_ss.at[n, k], a_rs.at[n, k], at_x(target + nx)[1])

    def activate(ch, scatters):
        gate_pre = x_sum(0, ch, scatters[0])
        up_pre = x_sum(1, ch, scatters[1])
        sigma = 1.0 / (1.0 + jnp.exp(-gate_pre))
        gate_factor = up_pre * sigma * (1.0 + gate_pre * (1.0 - sigma))
        up_factor = gate_pre * sigma
        hidden_grad = x_sum(2, ch, scatters[2])
        mine = shard_at(ch, 0)
        acts[ch * CORES + core, mine] = (hidden_grad * gate_factor).astype(BF)
        acts[(CHUNKS + ch) * CORES + core, mine] = (hidden_grad * up_factor).astype(BF)
        gathers = {}
        if nx > 1:
            for k in (2, nx - 2, 1, nx - 1):
                for a in range(2):
                    gathers[a, k] = gather_copy(a, ch, k, 0, k)
                    gathers[a, k].start()
        forwards = [to_sibling(a, ch, 0) for a in range(2)]
        return gathers, forwards

    def pass_on(ch, gathers, forwards):
        if nx == 1:
            return
        for k in (2, nx - 2):
            step = 1 if k == 2 else -1
            for a in range(2):
                gathers[a, k].wait_recv()
                if (a == 0) == (k == 2):
                    gathers[a, 4] = gather_copy(a, ch, 4, -2 * step, 2 * step)
                    gathers[a, 4].start()
                third = 3 if k == 2 else nx - 3
                gathers[a, third] = gather_copy(a, ch, third, -2 * step, step)
                gathers[a, third].start()
                forwards.append(to_sibling(a, ch, k))
        for k in (1, nx - 1, 3, nx - 3, 4):
            for a in range(2):
                gathers[a, k].wait_recv()
                forwards.append(to_sibling(a, ch, k))

    def give_back(ch, forwards):
        part = PARTS[ch]
        total = nz * part
        for copy in forwards:
            copy.wait_recv()
        value = None
        for a, w in ((0, w_gate), (1, w_up)):
            for c in range(CORES):
                act = acts[(a * CHUNKS + ch) * CORES + c, :total]
                term = mm_nt(act, w[:, c * half : (c + 1) * half])
                value = term if value is None else value + term
        back[ch, :total] = value.astype(BF)
        copies = {}
        for k in near_first(nz):
            t, device = at_z(k)
            copies[k] = remote(
                block(back, t, part, ch),
                block(zret, z, part, ch),
                b_ss.at[ch, k],
                b_rs.at[ch, k],
                device,
            )
            copies[k].start()
        at_mine = pl.ds(pl.multiple_of(z * part, 16), part)
        zret[ch, at_mine] = back[ch, at_mine]
        return copies

    starts = [sum(PARTS[:ch]) for ch in range(CHUNKS)]
    weights = ((0, w_gate), (0, w_up), (1, w_down_t))

    pack_rows(0, y_in)
    z_start(0, 0)
    pack_rows(1, y_gr)
    z_start(1, 0)
    z_pass(0, 0)
    cores = []
    scatters = [[] for _ in PARTS]
    gathers = [None] * CHUNKS
    forwards = [None] * CHUNKS
    z_back = []

    def scatter_forward(ch):
        if ch + 1 < CHUNKS:
            z_start(0, ch + 1)
        z_finish(0, ch)
        pair = [cores_send(p, ch, *weights[p]) for p in (0, 1)]
        z_pass(1, ch)
        if ch + 1 < CHUNKS:
            z_start(1, ch + 1)
        for p in (0, 1):
            scatters[ch].append(x_scatter(p, ch, *weights[p], pair[p]))
        cores.extend(pair)

    def scatter_down(ch):
        z_finish(1, ch)
        copy = cores_send(2, ch, *weights[2])
        if ch + 1 < CHUNKS:
            z_pass(0, ch + 1)
        x_combine(0, ch, scatters[ch][0])
        x_combine(1, ch, scatters[ch][1])
        scatters[ch].append(x_scatter(2, ch, *weights[2], copy))
        cores.append(copy)

    def gather(ch):
        gathers[ch], forwards[ch] = activate(ch, scatters[ch])

    for ch in range(CHUNKS):
        scatter_forward(ch)
        if ch > 0:
            gather(ch - 1)
        scatter_down(ch)
        if ch > 0:
            pass_on(ch - 1, gathers[ch - 1], forwards[ch - 1])
        x_combine(2, ch, scatters[ch][2])
        if ch > 0:
            z_back.append(give_back(ch - 1, forwards[ch - 1]))
    last = CHUNKS - 1
    gather(last)
    pass_on(last, gathers[last], forwards[last])
    z_back.append(give_back(last, forwards[last]))

    for a, grad in ((0, grad_gate), (1, grad_up)):
        for c in range(CORES):
            value = None
            for ch in range(CHUNKS):
                total = nz * PARTS[ch]
                term = mm_tn(rows[ch, :total], acts[(a * CHUNKS + ch) * CORES + c, :total])
                value = term if value is None else value + term
            grad[:, c * half : (c + 1) * half] = value.astype(BF)

    spread = None
    for ch in range(CHUNKS):
        arrived(z_back[ch])
        for g in range(groups):
            value = None
            for q in range(HSPLIT):
                part = PARTS[ch]
                first = (g * HSPLIT + q) * part
                term = zret[ch, first : first + part].astype(F32)
                value = term if value is None else value + term
            first = g * per_z + starts[ch]
            term = mm(unpack[:, first : first + part], value.astype(BF))
            spread = term if spread is None else spread + term
    yback[...] = spread.astype(BF)
    y_back = {}
    for k in near_first(ny):
        t, device = at_y(k)
        y_back[k] = remote(block(yback, t, blk), block(yret, y, blk), e_ss.at[k], e_rs.at[k], device)
        y_back[k].start()
    here = pl.ds(pl.multiple_of(y * blk, 16), blk)
    yret[here] = yback[here]
    arrived(y_back)
    in_grad_t[...] = mm_tn(yret[...], pick[...]).astype(BF)

    for a in range(2):
        for ch in range(CHUNKS):
            z_sent(a * CHUNKS + ch, ch)
    flat = [y_in, y_gr, y_back, *z_back, *gathers]
    for each in scatters:
        flat.extend(each)
    for copies in flat:
        for copy in copies.values():
            copy.wait_send()
    for copy in cores:
        copy.wait_send()
    for each in forwards:
        for copy in each:
            copy.wait_send()


def per_device(sizes, out_grad, inputs, expert_ids, gate_weights, w_gate, w_up, w_down):
    nx, ny, nz = sizes
    tokens, feature = out_grad.shape
    hidden = w_gate.shape[1]
    half = hidden // CORES
    groups = nz // HSPLIT
    slots = ny * groups * SLOT
    per_z = ny * CAP
    part = max(PARTS)
    total = nz * part
    shard = total // nx
    dma = pltpu.SemaphoreType.DMA
    vmem = pltpu.VMEM
    in_grad_t, grad_gate, grad_up = pl.pallas_call(
        functools.partial(kernel, sizes),
        out_shape=(
            jax.ShapeDtypeStruct((feature, tokens), BF),
            jax.ShapeDtypeStruct((feature, hidden), BF),
            jax.ShapeDtypeStruct((feature, hidden), BF),
        ),
        in_specs=[pl.BlockSpec(memory_space=vmem)] * 7,
        out_specs=(pl.BlockSpec(memory_space=vmem),) * 3,
        scratch_shapes=[
            vmem((slots, tokens), BF),
            vmem((2, slots, feature), BF),
            vmem((2, slots, feature), BF),
            vmem((2 * CHUNKS * groups, part, feature), BF),
            vmem((2 * CHUNKS, total, feature), BF),
            vmem((3 * CHUNKS, total, half), BF),
            vmem((3 * CHUNKS, total, half), BF),
            vmem((3 * CHUNKS, total, half), F32),
            vmem((3 * CHUNKS, total, half), BF),
            vmem((3 * CHUNKS, 7, shard, half), BF),
            vmem((3 * CHUNKS, 2, shard, half), BF),
            vmem((2 * CHUNKS * CORES, total, half), BF),
            vmem((CHUNKS, total, feature), BF),
            vmem((CHUNKS, total, feature), BF),
            vmem((slots, feature), BF),
            vmem((slots, feature), BF),
            dma((2, ny)),
            dma((2, ny)),
            dma((2 * CHUNKS, 8)),
            dma((2 * CHUNKS, nz)),
            dma((3 * CHUNKS,)),
            dma((3 * CHUNKS,)),
            dma((3 * CHUNKS, 7)),
            dma((3 * CHUNKS, 7)),
            dma((2 * CHUNKS, nx)),
            dma((2 * CHUNKS, nx)),
            dma((2 * CHUNKS, nx)),
            dma((2 * CHUNKS, nx)),
            dma((CHUNKS, nz)),
            dma((CHUNKS, nz)),
            dma((ny,)),
            dma((ny,)),
        ],
        compiler_params=pltpu.CompilerParams(
            collective_id=0, has_side_effects=True, vmem_limit_bytes=48 * 1024 * 1024
        ),
        cost_estimate=pl.CostEstimate(
            flops=14 * nz * per_z * feature * hidden, bytes_accessed=4_000_000, transcendentals=0
        ),
    )(out_grad.T, inputs.T, expert_ids.T, gate_weights.T, w_gate, w_up, w_down.T)
    return in_grad_t.T, grad_gate, grad_up


def solution(mesh, sizes=None):
    if sizes is None:
        ny, nz = grid_of(mesh.shape["expert"])
        sizes = (mesh.shape["dp"] // CORES, ny, nz)
    placed = (
        P("expert", "dp"),
        P("expert", "dp"),
        P("expert", None),
        P("expert", None),
        P("dp", "expert"),
        P("dp", "expert"),
        P("expert", "dp"),
    )
    return jax.shard_map(
        functools.partial(per_device, sizes),
        mesh=mesh,
        in_specs=placed,
        out_specs=(P("expert", "dp"), P("dp", "expert"), P("dp", "expert")),
        check_vma=False,
    )
```

```python
import functools

import jax
import jax.numpy as jnp
from jax import lax
from jax.experimental import pallas as pl
from jax.experimental.pallas import tpu as pltpu
from jax.sharding import PartitionSpec as P

HSPLIT = 4
CAP = 12
SLOT = 16
PARTS = (48, 48)
CHUNKS = len(PARTS)
Z_FIRST = (
    ((0, 1), (1, 1), (1, 3)),
    ((0, 2), (1, 3), (1, 0), (0, 0)),
    ((0, 1), (1, 0), (1, 3), (0, 3)),
    ((0, 2), (1, 2), (1, 0)),
)
Z_SECOND = (
    ((7, 1), (6, 1), (5, 1)),
    ((0, 3), (0, 2), (4, 0), (2, 0)),
    ((3, 0), (3, 1), (7, 3), (1, 3)),
    ((4, 2), (5, 2), (6, 2)),
)
CORES = 2
BF = jnp.bfloat16
F32 = jnp.float32


def grid_of(devices):
    side = 1
    while side * side < devices:
        side *= 2
    return devices // side, side


def mm(a, b):
    return lax.dot_general(a, b, (((1,), (0,)), ((), ())), preferred_element_type=F32)


def mm_nt(a, b):
    return lax.dot_general(a, b, (((1,), (1,)), ((), ())), preferred_element_type=F32)


def mm_tn(a, b):
    return lax.dot_general(a, b, (((0,), (0,)), ((), ())), preferred_element_type=F32)


def iota(shape, dim):
    return lax.broadcasted_iota(jnp.int32, shape, dim)


def near_first(n):
    order = []
    for k in range(1, n // 2 + 1):
        order.append(k)
        if n - k != k:
            order.append(n - k)
    return order


def kernel(
    sizes,
    out_grad_h,
    inputs_h,
    ids_h,
    gates_h,
    w_gate_h,
    w_up_h,
    w_down_h,
    in_grad_h,
    grad_gate_h,
    grad_up_h,
    in_grad_t,
    grad_gate,
    grad_up,
    out_grad_t,
    inputs_t,
    ids_t,
    gates_t,
    w_gate,
    w_up,
    w_down_t,
    pick,
    ysend,
    yrecv,
    zsend,
    rows,
    csend,
    crecv,
    own,
    rsend,
    rrecv,
    xcomb,
    acts,
    back,
    zret,
    yback,
    yret,
    y_ss,
    y_rs,
    z_ss,
    z_rs,
    c_ss,
    c_rs,
    r_ss,
    r_rs,
    a_ss,
    a_rs,
    s_ss,
    s_rs,
    b_ss,
    b_rs,
    e_ss,
    e_rs,
    l_s,
):
    nx, ny, nz = sizes
    groups = nz // HSPLIT
    blk = groups * SLOT
    slots = ny * blk
    per_z = ny * CAP
    tokens = ids_t.shape[1]
    half = w_gate.shape[1] // CORES

    dp = lax.axis_index("dp")
    ex = lax.axis_index("expert")
    x, core = dp // CORES, dp % CORES
    y, z = ex // nz, ex % nz
    zgroup = z // HSPLIT
    sibling = (x * CORES + 1 - core, ex)

    def at_y(k):
        t = (y + k) % ny
        return t, (dp, t * nz + z)

    def at_z(k):
        t = (z + k) % nz
        return t, (dp, y * nz + t)

    def at_x(k):
        t = (x + k) % nx
        return t, (t * CORES + core, ex)

    def remote(src, dst, ssem, rsem, device):
        return pltpu.make_async_remote_copy(
            src_ref=src,
            dst_ref=dst,
            send_sem=ssem,
            recv_sem=rsem,
            device_id=device,
            device_id_type=pl.DeviceIdType.MESH,
        )

    loads = {}
    for name, (source, target) in dict(
        ids=(ids_h, ids_t),
        inputs=(inputs_h, inputs_t),
        gates=(gates_h, gates_t),
        out_grad=(out_grad_h, out_grad_t),
        w_gate=(w_gate_h, w_gate),
        w_up=(w_up_h, w_up),
        w_down=(w_down_h, w_down_t),
    ).items():
        loads[name] = pltpu.make_async_copy(source, target, l_s.at[len(loads)])
        loads[name].start()

    partners = (
        [at_y(k)[1] for k in range(1, ny)]
        + [at_z(k)[1] for k in range(1, nz)]
        + [at_x(k)[1] for k in range(1, nx)]
        + [sibling]
    )
    barrier = pltpu.get_barrier_semaphore()
    for device in partners:
        pl.semaphore_signal(barrier, inc=1, device_id=device, device_id_type=pl.DeviceIdType.MESH)

    expert = iota((128, tokens), 0)
    hits = jnp.zeros((128, tokens), F32)
    loads["ids"].wait()
    loads["gates"].wait()
    gate = jnp.zeros((128, tokens), F32)
    for k in range(ids_t.shape[0]):
        hit = ids_t[k : k + 1, :] == expert
        hits = hits + jnp.where(hit, 1.0, 0.0)
        gate = gate + jnp.where(hit, gates_t[k : k + 1, :], 0.0)
    hits_b = hits.astype(BF)
    before = jnp.where(iota((tokens, tokens), 0) < iota((tokens, tokens), 1), 1.0, 0.0).astype(BF)
    slot_of = mm(hits_b, before).astype(BF)
    expand = jnp.where(iota((slots, 128), 0) // SLOT == iota((slots, 128), 1), 1.0, 0.0).astype(BF)
    hit_rt = mm(expand, hits_b)
    slot_rt = mm(expand, slot_of)
    wanted = (iota((slots, tokens), 0) % SLOT).astype(F32)
    picker = jnp.where(jnp.logical_and(hit_rt > 0.5, slot_rt == wanted), 1.0, 0.0)
    picker_b = picker.astype(BF)
    pick[...] = picker_b

    def block(ref, index, count, *lead):
        return ref.at[(*lead, pl.ds(pl.multiple_of(index * count, 16), count))]

    def y_copies(a):
        copies = {}
        for k in near_first(ny):
            t, device = at_y(k)
            copies[k] = remote(
                block(ysend, t, blk, a),
                block(yrecv, y, blk, a),
                y_ss.at[a, k],
                y_rs.at[a, k],
                device,
            )
            copies[k].start()
        return copies

    loads["inputs"].wait()
    ysend[0] = mm_nt(picker_b, inputs_t[...]).astype(BF)
    pl.semaphore_wait(barrier, len(partners))
    y_in = y_copies(0)
    gate_1 = gate.astype(BF)
    rest = gate - gate_1.astype(F32)
    gate_2 = rest.astype(BF)
    gate_3 = (rest - gate_2.astype(F32)).astype(BF)
    gate_rt = mm(expand, gate_1) + mm(expand, gate_2) + mm(expand, gate_3)
    scale = jnp.sum(picker * gate_rt, axis=1, keepdims=True)
    loads["out_grad"].wait()
    ysend[1] = (scale * mm_nt(picker_b, out_grad_t[...])).astype(BF)
    y_gr = y_copies(1)

    def turn(value):
        return value % 2 * (ny // 2) + value // 2

    col = iota((groups * per_z, slots), 1)
    seat = (col // SLOT % groups) * per_z + turn(col // blk) * CAP + col % SLOT
    pack = jnp.where(
        jnp.logical_and(seat == iota((groups * per_z, slots), 0), col % SLOT < CAP), 1.0, 0.0
    ).astype(BF)
    row = iota((slots, groups * per_z), 0)
    seat_t = (row // SLOT % groups) * per_z + turn(row // blk) * CAP + row % SLOT
    unpack = jnp.where(
        jnp.logical_and(seat_t == iota((slots, groups * per_z), 1), row % SLOT < CAP), 1.0, 0.0
    ).astype(BF)

    def arrived(copies):
        for copy in copies.values():
            copy.wait_recv()

    def pack_rows(a, y_in_flight):
        here = pl.ds(pl.multiple_of(y * blk, 16), blk)
        yrecv[a, here] = ysend[a, here]
        arrived(y_in_flight)
        packed = mm(pack, yrecv[a]).astype(BF)
        for g in range(groups):
            for ch in range(CHUNKS):
                first = g * per_z + starts[ch]
                zsend[(a * CHUNKS + ch) * groups + g, : PARTS[ch]] = packed[
                    first : first + PARTS[ch]
                ]

    place = z % HSPLIT

    def z_device(other, to):
        group = 1 - zgroup if other else zgroup
        return (dp, y * nz + group * HSPLIT + to)

    def z_rows(n, ch, source):
        return block(rows, source, PARTS[ch], n)

    def z_source(tag):
        group = 1 - zgroup if tag >= HSPLIT else zgroup
        return group * HSPLIT + tag % HSPLIT

    def z_first(n, ch, at, j):
        other, to = Z_FIRST[at][j]
        group = 1 - zgroup if other else zgroup
        tag = at + HSPLIT * other
        return remote(
            zsend.at[n * groups + group, pl.ds(0, PARTS[ch])],
            z_rows(n, ch, z),
            z_ss.at[n, j],
            z_rs.at[n, tag],
            z_device(other, to),
        )

    def z_second(n, ch, at, j):
        tag, to = Z_SECOND[at][j]
        view = z_rows(n, ch, z_source(tag))
        return remote(view, view, z_ss.at[n, 4 + j], z_rs.at[n, tag], z_device(False, to))

    def z_arrival(n, ch, tag):
        view = z_rows(n, ch, z_source(tag))
        remote(view, view, z_ss.at[n, 0], z_rs.at[n, tag], sibling).wait_recv()

    def each_place(step):
        for at in range(HSPLIT):
            pl.when(place == at)(functools.partial(step, at))

    def z_start(a, ch):
        n = a * CHUNKS + ch
        part = PARTS[ch]

        def step(at):
            for j in range(len(Z_FIRST[at])):
                z_first(n, ch, at, j).start()

        each_place(step)
        rows[n, pl.ds(pl.multiple_of(z * part, 16), part)] = zsend[n * groups + zgroup, :part]

    def z_pass(a, ch):
        n = a * CHUNKS + ch

        def step(at):
            done = []
            for j, (tag, _) in enumerate(Z_SECOND[at]):
                if tag not in done:
                    z_arrival(n, ch, tag)
                    done.append(tag)
                z_second(n, ch, at, j).start()

        each_place(step)

    def z_finish(a, ch):
        n = a * CHUNKS + ch

        def step(at):
            passed = [tag for tag, _ in Z_SECOND[at]]
            for tag in range(nz):
                if tag != at and tag not in passed:
                    z_arrival(n, ch, tag)

        each_place(step)

    def z_sent(n, ch):
        def step(at):
            for j in range(len(Z_FIRST[at])):
                z_first(n, ch, at, j).wait_send()
            for j in range(len(Z_SECOND[at])):
                z_second(n, ch, at, j).wait_send()

        each_place(step)

    def product(a, ch, w, mine):
        start = pl.multiple_of((core if mine else 1 - core) * half, 128)
        return mm(rows[a * CHUNKS + ch, : nz * PARTS[ch]], w[:, pl.ds(start, half)])

    def cores_send(p, ch, a, w):
        n = p * CHUNKS + ch
        total = nz * PARTS[ch]
        csend[n, :total] = product(a, ch, w, False).astype(BF)
        at = pl.ds(0, total)
        copy = remote(csend.at[n, at], crecv.at[n, at], c_ss.at[n], c_rs.at[n], sibling)
        copy.start()
        return copy

    def shard_at(ch, k):
        shard = nz * PARTS[ch] // nx
        return pl.ds(pl.multiple_of((x + nx + k) % nx * shard, 16), shard)

    def x_copy(n, ch, role, source, k):
        where = pl.ds(0, nz * PARTS[ch] // nx)
        return remote(
            source, rrecv.at[n, role, where], r_ss.at[n, role], r_rs.at[n, role], at_x(k + nx)[1]
        )

    def x_scatter(p, ch, a, w, core_copy):
        n = p * CHUNKS + ch
        total = nz * PARTS[ch]
        value = product(a, ch, w, True)
        core_copy.wait_recv()
        value = value + crecv[n, :total].astype(F32)
        own[n, :total] = value
        rsend[n, :total] = value.astype(BF)
        copies = {}
        if nx > 1:
            far = 2 if (p + ch) % 2 == 0 else -2
            for role, shard, k in ((4, 4, far), (2, 3, 1), (3, -3, -1), (0, 1, 1), (1, -1, -1)):
                copies[role] = x_copy(n, ch, role, rsend.at[n, shard_at(ch, shard)], k)
                copies[role].start()
        return copies

    def x_combine(p, ch, copies):
        n = p * CHUNKS + ch
        shard = nz * PARTS[ch] // nx
        if nx > 1:
            even = (p + ch) % 2 == 0
            copies[2].wait_recv()
            copies[3].wait_recv()
            copies[4].wait_recv()
            for i, k in ((0, 2), (1, -2)) if even else ((1, -2), (0, 2)):
                value = own[n, shard_at(ch, k)] + rrecv[n, 2 + i, :shard].astype(F32)
                if even == (i == 0):
                    value = value + rrecv[n, 4, :shard].astype(F32)
                xcomb[n, i, :shard] = value.astype(BF)
                copies[5 + i] = x_copy(n, ch, 5 + i, xcomb.at[n, i, pl.ds(0, shard)], k)
                copies[5 + i].start()

    def x_sum(p, ch, copies):
        n = p * CHUNKS + ch
        shard = nz * PARTS[ch] // nx
        value = own[n, shard_at(ch, 0)]
        for role in (0, 1, 5, 6) if nx > 1 else ():
            copies[role].wait_recv()
            value = value + rrecv[n, role, :shard].astype(F32)
        return value

    def act_view(a, ch, k):
        return acts.at[(a * CHUNKS + ch) * CORES + core, shard_at(ch, k)]

    def to_sibling(a, ch, k):
        n = a * CHUNKS + ch
        view = act_view(a, ch, -k)
        copy = remote(view, view, s_ss.at[n, k], s_rs.at[n, k], sibling)
        copy.start()
        return copy

    def gather_copy(a, ch, k, away, target):
        n = a * CHUNKS + ch
        view = act_view(a, ch, away)
        return remote(view, view, a_ss.at[n, k], a_rs.at[n, k], at_x(target + nx)[1])

    def activate(ch, scatters):
        gate_pre = x_sum(0, ch, scatters[0])
        up_pre = x_sum(1, ch, scatters[1])
        sigma = 1.0 / (1.0 + jnp.exp(-gate_pre))
        gate_factor = up_pre * sigma * (1.0 + gate_pre * (1.0 - sigma))
        up_factor = gate_pre * sigma
        hidden_grad = x_sum(2, ch, scatters[2])
        mine = shard_at(ch, 0)
        acts[ch * CORES + core, mine] = (hidden_grad * gate_factor).astype(BF)
        acts[(CHUNKS + ch) * CORES + core, mine] = (hidden_grad * up_factor).astype(BF)
        gathers = {}
        if nx > 1:
            for k in (2, nx - 2, 1, nx - 1):
                for a in range(2):
                    gathers[a, k] = gather_copy(a, ch, k, 0, k)
                    gathers[a, k].start()
        forwards = [to_sibling(a, ch, 0) for a in range(2)]
        return gathers, forwards

    def pass_on(ch, gathers, forwards):
        if nx == 1:
            return
        for k in (2, nx - 2):
            step = 1 if k == 2 else -1
            for a in range(2):
                gathers[a, k].wait_recv()
                if (a == 0) == (k == 2):
                    gathers[a, 4] = gather_copy(a, ch, 4, -2 * step, 2 * step)
                    gathers[a, 4].start()
                third = 3 if k == 2 else nx - 3
                gathers[a, third] = gather_copy(a, ch, third, -2 * step, step)
                gathers[a, third].start()
                forwards.append(to_sibling(a, ch, k))

    def pass_rest(ch, gathers, forwards):
        if nx == 1:
            return
        for k in (1, nx - 1, 3, nx - 3, 4):
            for a in range(2):
                gathers[a, k].wait_recv()
                forwards.append(to_sibling(a, ch, k))

    def give_back(ch, forwards):
        part = PARTS[ch]
        total = nz * part
        for copy in forwards:
            copy.wait_recv()
        value = None
        for a, w in ((0, w_gate), (1, w_up)):
            for c in range(CORES):
                act = acts[(a * CHUNKS + ch) * CORES + c, :total]
                term = mm_nt(act, w[:, c * half : (c + 1) * half])
                value = term if value is None else value + term
        back[ch, :total] = value.astype(BF)
        copies = {}
        for k in near_first(nz):
            t, device = at_z(k)
            copies[k] = remote(
                block(back, t, part, ch),
                block(zret, z, part, ch),
                b_ss.at[ch, k],
                b_rs.at[ch, k],
                device,
            )
            copies[k].start()
        at_mine = pl.ds(pl.multiple_of(z * part, 16), part)
        zret[ch, at_mine] = back[ch, at_mine]
        return copies

    starts = [sum(PARTS[:ch]) for ch in range(CHUNKS)]
    weights = ((0, w_gate), (0, w_up), (1, w_down_t))

    pack_rows(0, y_in)
    z_start(0, 0)
    pack_rows(1, y_gr)
    z_start(1, 0)
    z_pass(0, 0)
    for name in ("w_gate", "w_up", "w_down"):
        loads[name].wait()
    cores = []
    scatters = [[] for _ in PARTS]
    gathers = [None] * CHUNKS
    forwards = [None] * CHUNKS
    z_back = []

    def scatter_forward(ch):
        if ch + 1 < CHUNKS:
            z_start(0, ch + 1)
        z_finish(0, ch)
        pair = [cores_send(p, ch, *weights[p]) for p in (0, 1)]
        z_pass(1, ch)
        if ch + 1 < CHUNKS:
            z_start(1, ch + 1)
        for p in (0, 1):
            scatters[ch].append(x_scatter(p, ch, *weights[p], pair[p]))
        cores.extend(pair)

    def scatter_down(ch):
        z_finish(1, ch)
        copy = cores_send(2, ch, *weights[2])
        if ch + 1 < CHUNKS:
            z_pass(0, ch + 1)
        x_combine(0, ch, scatters[ch][0])
        x_combine(1, ch, scatters[ch][1])
        scatters[ch].append(x_scatter(2, ch, *weights[2], copy))
        cores.append(copy)

    def gather(ch):
        gathers[ch], forwards[ch] = activate(ch, scatters[ch])

    for ch in range(CHUNKS):
        scatter_forward(ch)
        if ch > 0:
            gather(ch - 1)
        scatter_down(ch)
        if ch > 0:
            pass_on(ch - 1, gathers[ch - 1], forwards[ch - 1])
        x_combine(2, ch, scatters[ch][2])
        if ch > 0:
            pass_rest(ch - 1, gathers[ch - 1], forwards[ch - 1])
            z_back.append(give_back(ch - 1, forwards[ch - 1]))
    last = CHUNKS - 1
    gather(last)
    pass_on(last, gathers[last], forwards[last])
    pass_rest(last, gathers[last], forwards[last])
    z_back.append(give_back(last, forwards[last]))

    for a, grad in ((0, grad_gate), (1, grad_up)):
        for c in range(CORES):
            value = None
            for ch in range(CHUNKS):
                total = nz * PARTS[ch]
                term = mm_tn(rows[ch, :total], acts[(a * CHUNKS + ch) * CORES + c, :total])
                value = term if value is None else value + term
            grad[:, c * half : (c + 1) * half] = value.astype(BF)

    stores = []
    for source, target in ((grad_gate, grad_gate_h), (grad_up, grad_up_h)):
        stores.append(pltpu.make_async_copy(source, target, l_s.at[len(loads) + len(stores)]))
        stores[-1].start()
    y_back = {}
    for k in near_first(ny):
        t, device = at_y(k)
        y_back[k] = remote(block(yback, t, blk), block(yret, y, blk), e_ss.at[k], e_rs.at[k], device)

    for ch in range(CHUNKS):
        arrived(z_back[ch])
        part = PARTS[ch]
        spread = None
        for g in range(groups):
            value = None
            for q in range(HSPLIT):
                first = (g * HSPLIT + q) * part
                term = zret[ch, first : first + part].astype(F32)
                value = term if value is None else value + term
            first = g * per_z + starts[ch]
            term = mm(unpack[:, first : first + part], value.astype(BF))
            spread = term if spread is None else spread + term
        spread = spread.astype(BF)
        for t in range(ch, ny, CHUNKS):
            yback[t * blk : (t + 1) * blk] = spread[t * blk : (t + 1) * blk]

        def step(parity):
            for k in near_first(ny):
                if (k + parity) % 2 == ch:
                    y_back[k].start()

        for parity in range(2):
            pl.when(y % 2 == parity)(functools.partial(step, parity))
    here = pl.ds(pl.multiple_of(y * blk, 16), blk)
    yret[here] = yback[here]
    arrived(y_back)
    in_grad_t[...] = mm_tn(yret[...], pick[...]).astype(BF)
    stores.append(pltpu.make_async_copy(in_grad_t, in_grad_h, l_s.at[len(loads) + len(stores)]))
    stores[-1].start()

    for a in range(2):
        for ch in range(CHUNKS):
            z_sent(a * CHUNKS + ch, ch)
    for copy in stores:
        copy.wait()
    flat = [y_in, y_gr, y_back, *z_back, *gathers]
    for each in scatters:
        flat.extend(each)
    for copies in flat:
        for copy in copies.values():
            copy.wait_send()
    for copy in cores:
        copy.wait_send()
    for each in forwards:
        for copy in each:
            copy.wait_send()


def per_device(sizes, out_grad, inputs, expert_ids, gate_weights, w_gate, w_up, w_down):
    nx, ny, nz = sizes
    tokens, feature = out_grad.shape
    hidden = w_gate.shape[1]
    half = hidden // CORES
    groups = nz // HSPLIT
    slots = ny * groups * SLOT
    per_z = ny * CAP
    part = max(PARTS)
    total = nz * part
    shard = total // nx
    dma = pltpu.SemaphoreType.DMA
    vmem = pltpu.VMEM
    in_grad_t, grad_gate, grad_up = pl.pallas_call(
        functools.partial(kernel, sizes),
        out_shape=(
            jax.ShapeDtypeStruct((feature, tokens), BF),
            jax.ShapeDtypeStruct((feature, hidden), BF),
            jax.ShapeDtypeStruct((feature, hidden), BF),
        ),
        in_specs=[pl.BlockSpec(memory_space=pltpu.HBM)] * 7,
        out_specs=(pl.BlockSpec(memory_space=pltpu.HBM),) * 3,
        scratch_shapes=[
            vmem((feature, tokens), BF),
            vmem((feature, hidden), BF),
            vmem((feature, hidden), BF),
            vmem((feature, tokens), BF),
            vmem((feature, tokens), BF),
            vmem((expert_ids.shape[1], tokens), jnp.int32),
            vmem((expert_ids.shape[1], tokens), F32),
            vmem((feature, hidden), BF),
            vmem((feature, hidden), BF),
            vmem((feature, hidden), BF),
            vmem((slots, tokens), BF),
            vmem((2, slots, feature), BF),
            vmem((2, slots, feature), BF),
            vmem((2 * CHUNKS * groups, part, feature), BF),
            vmem((2 * CHUNKS, total, feature), BF),
            vmem((3 * CHUNKS, total, half), BF),
            vmem((3 * CHUNKS, total, half), BF),
            vmem((3 * CHUNKS, total, half), F32),
            vmem((3 * CHUNKS, total, half), BF),
            vmem((3 * CHUNKS, 7, shard, half), BF),
            vmem((3 * CHUNKS, 2, shard, half), BF),
            vmem((2 * CHUNKS * CORES, total, half), BF),
            vmem((CHUNKS, total, feature), BF),
            vmem((CHUNKS, total, feature), BF),
            vmem((slots, feature), BF),
            vmem((slots, feature), BF),
            dma((2, ny)),
            dma((2, ny)),
            dma((2 * CHUNKS, 8)),
            dma((2 * CHUNKS, nz)),
            dma((3 * CHUNKS,)),
            dma((3 * CHUNKS,)),
            dma((3 * CHUNKS, 7)),
            dma((3 * CHUNKS, 7)),
            dma((2 * CHUNKS, nx)),
            dma((2 * CHUNKS, nx)),
            dma((2 * CHUNKS, nx)),
            dma((2 * CHUNKS, nx)),
            dma((CHUNKS, nz)),
            dma((CHUNKS, nz)),
            dma((ny,)),
            dma((ny,)),
            dma((10,)),
        ],
        compiler_params=pltpu.CompilerParams(
            collective_id=0, has_side_effects=True, vmem_limit_bytes=56 * 1024 * 1024
        ),
        cost_estimate=pl.CostEstimate(
            flops=14 * nz * per_z * feature * hidden, bytes_accessed=4_000_000, transcendentals=0
        ),
    )(out_grad.T, inputs.T, expert_ids.T, gate_weights.T, w_gate, w_up, w_down.T)
    return in_grad_t.T, grad_gate, grad_up


def solution(mesh, sizes=None):
    if sizes is None:
        ny, nz = grid_of(mesh.shape["expert"])
        sizes = (mesh.shape["dp"] // CORES, ny, nz)
    placed = (
        P("expert", "dp"),
        P("expert", "dp"),
        P("expert", None),
        P("expert", None),
        P("dp", "expert"),
        P("dp", "expert"),
        P("expert", "dp"),
    )
    return jax.shard_map(
        functools.partial(per_device, sizes),
        mesh=mesh,
        in_specs=placed,
        out_specs=(P("expert", "dp"), P("dp", "expert"), P("dp", "expert")),
        check_vma=False,
    )
```

```python
import functools

import jax
import jax.numpy as jnp
from jax import lax
from jax.experimental import pallas as pl
from jax.experimental.pallas import tpu as pltpu
from jax.sharding import PartitionSpec as P

HSPLIT = 4
CAP = 12
SLOT = 16
PARTS = (48, 48)
CHUNKS = len(PARTS)
Z_FIRST = (
    ((0, 1), (1, 1), (1, 3)),
    ((0, 2), (1, 3), (1, 0), (0, 0)),
    ((0, 1), (1, 0), (1, 3), (0, 3)),
    ((0, 2), (1, 2), (1, 0)),
)
Z_SECOND = (
    ((7, 1), (6, 1), (5, 1)),
    ((0, 3), (0, 2), (4, 0), (2, 0)),
    ((3, 0), (3, 1), (7, 3), (1, 3)),
    ((4, 2), (5, 2), (6, 2)),
)
CORES = 2
BF = jnp.bfloat16
F32 = jnp.float32


def relay_tags(at):
    return list(dict.fromkeys(tag for tag, _ in Z_SECOND[at]))


def back_sends(at):
    plan = []
    for relay in range(HSPLIT):
        for j, (tag, to) in enumerate(Z_SECOND[relay]):
            if to == at:
                plan.append((tag, False, relay, 4 + j))
    for home in range(HSPLIT):
        for j, (other, to) in enumerate(Z_FIRST[home]):
            tag = home + HSPLIT * other
            if to == at and tag not in relay_tags(at):
                plan.append((tag, other == 1, home, j))
    return plan


def back_relays(at):
    plan = []
    for tag in relay_tags(at):
        parts = [j for j, (each, _) in enumerate(Z_SECOND[at]) if each == tag]
        home, other = tag % HSPLIT, tag // HSPLIT
        plan.append((tag, parts, other == 1, home, Z_FIRST[home].index((other, at))))
    return plan


def grid_of(devices):
    side = 1
    while side * side < devices:
        side *= 2
    return devices // side, side


def mm(a, b):
    return lax.dot_general(a, b, (((1,), (0,)), ((), ())), preferred_element_type=F32)


def mm_nt(a, b):
    return lax.dot_general(a, b, (((1,), (1,)), ((), ())), preferred_element_type=F32)


def mm_tn(a, b):
    return lax.dot_general(a, b, (((0,), (0,)), ((), ())), preferred_element_type=F32)


def iota(shape, dim):
    return lax.broadcasted_iota(jnp.int32, shape, dim)


def near_first(n):
    order = []
    for k in range(1, n // 2 + 1):
        order.append(k)
        if n - k != k:
            order.append(n - k)
    return order


def kernel(
    sizes,
    out_grad_h,
    inputs_h,
    ids_h,
    gates_h,
    w_gate_h,
    w_up_h,
    w_down_h,
    in_grad_h,
    grad_gate_h,
    grad_up_h,
    in_grad_t,
    grad_gate,
    grad_up,
    out_grad_t,
    inputs_t,
    ids_t,
    gates_t,
    w_gate,
    w_up,
    w_down_t,
    pick,
    ysend,
    yrecv,
    zsend,
    rows,
    csend,
    crecv,
    own,
    rsend,
    rrecv,
    xcomb,
    acts,
    back,
    zret,
    zcomb,
    zsum,
    yback,
    yret,
    y_ss,
    y_rs,
    z_ss,
    z_rs,
    c_ss,
    c_rs,
    r_ss,
    r_rs,
    a_ss,
    a_rs,
    s_ss,
    s_rs,
    b_ss,
    b_rs,
    e_ss,
    e_rs,
    l_s,
):
    nx, ny, nz = sizes
    groups = nz // HSPLIT
    blk = groups * SLOT
    slots = ny * blk
    per_z = ny * CAP
    tokens = ids_t.shape[1]
    half = w_gate.shape[1] // CORES

    dp = lax.axis_index("dp")
    ex = lax.axis_index("expert")
    x, core = dp // CORES, dp % CORES
    y, z = ex // nz, ex % nz
    zgroup = z // HSPLIT
    sibling = (x * CORES + 1 - core, ex)

    def at_y(k):
        t = (y + k) % ny
        return t, (dp, t * nz + z)

    def at_z(k):
        t = (z + k) % nz
        return t, (dp, y * nz + t)

    def at_x(k):
        t = (x + k) % nx
        return t, (t * CORES + core, ex)

    def remote(src, dst, ssem, rsem, device):
        return pltpu.make_async_remote_copy(
            src_ref=src,
            dst_ref=dst,
            send_sem=ssem,
            recv_sem=rsem,
            device_id=device,
            device_id_type=pl.DeviceIdType.MESH,
        )

    loads = {}
    for name, (source, target) in dict(
        ids=(ids_h, ids_t),
        inputs=(inputs_h, inputs_t),
        gates=(gates_h, gates_t),
        out_grad=(out_grad_h, out_grad_t),
        w_gate=(w_gate_h, w_gate),
        w_up=(w_up_h, w_up),
        w_down=(w_down_h, w_down_t),
    ).items():
        loads[name] = pltpu.make_async_copy(source, target, l_s.at[len(loads)])
        loads[name].start()

    partners = (
        [at_y(k)[1] for k in range(1, ny)]
        + [at_z(k)[1] for k in range(1, nz)]
        + [at_x(k)[1] for k in range(1, nx)]
        + [sibling]
    )
    barrier = pltpu.get_barrier_semaphore()
    for device in partners:
        pl.semaphore_signal(barrier, inc=1, device_id=device, device_id_type=pl.DeviceIdType.MESH)

    expert = iota((128, tokens), 0)
    hits = jnp.zeros((128, tokens), F32)
    loads["ids"].wait()
    loads["gates"].wait()
    gate = jnp.zeros((128, tokens), F32)
    for k in range(ids_t.shape[0]):
        hit = ids_t[k : k + 1, :] == expert
        hits = hits + jnp.where(hit, 1.0, 0.0)
        gate = gate + jnp.where(hit, gates_t[k : k + 1, :], 0.0)
    hits_b = hits.astype(BF)
    before = jnp.where(iota((tokens, tokens), 0) < iota((tokens, tokens), 1), 1.0, 0.0).astype(BF)
    slot_of = mm(hits_b, before).astype(BF)
    expand = jnp.where(iota((slots, 128), 0) // SLOT == iota((slots, 128), 1), 1.0, 0.0).astype(BF)
    hit_rt = mm(expand, hits_b)
    slot_rt = mm(expand, slot_of)
    wanted = (iota((slots, tokens), 0) % SLOT).astype(F32)
    picker = jnp.where(jnp.logical_and(hit_rt > 0.5, slot_rt == wanted), 1.0, 0.0)
    picker_b = picker.astype(BF)
    pick[...] = picker_b

    def block(ref, index, count, *lead):
        return ref.at[(*lead, pl.ds(pl.multiple_of(index * count, 16), count))]

    def y_copies(a):
        copies = {}
        for k in near_first(ny):
            t, device = at_y(k)
            copies[k] = remote(
                block(ysend, t, blk, a),
                block(yrecv, y, blk, a),
                y_ss.at[a, k],
                y_rs.at[a, k],
                device,
            )
            copies[k].start()
        return copies

    loads["inputs"].wait()
    ysend[0] = mm_nt(picker_b, inputs_t[...]).astype(BF)
    pl.semaphore_wait(barrier, len(partners))
    y_in = y_copies(0)
    gate_1 = gate.astype(BF)
    rest = gate - gate_1.astype(F32)
    gate_2 = rest.astype(BF)
    gate_3 = (rest - gate_2.astype(F32)).astype(BF)
    gate_rt = mm(expand, gate_1) + mm(expand, gate_2) + mm(expand, gate_3)
    scale = jnp.sum(picker * gate_rt, axis=1, keepdims=True)
    loads["out_grad"].wait()
    ysend[1] = (scale * mm_nt(picker_b, out_grad_t[...])).astype(BF)
    y_gr = y_copies(1)

    def turn(value):
        return value % 2 * (ny // 2) + value // 2

    col = iota((groups * per_z, slots), 1)
    seat = (col // SLOT % groups) * per_z + turn(col // blk) * CAP + col % SLOT
    pack = jnp.where(
        jnp.logical_and(seat == iota((groups * per_z, slots), 0), col % SLOT < CAP), 1.0, 0.0
    ).astype(BF)
    row = iota((slots, groups * per_z), 0)
    seat_t = (row // SLOT % groups) * per_z + turn(row // blk) * CAP + row % SLOT
    unpack = jnp.where(
        jnp.logical_and(seat_t == iota((slots, groups * per_z), 1), row % SLOT < CAP), 1.0, 0.0
    ).astype(BF)

    def arrived(copies):
        for copy in copies.values():
            copy.wait_recv()

    def pack_rows(a, y_in_flight):
        here = pl.ds(pl.multiple_of(y * blk, 16), blk)
        yrecv[a, here] = ysend[a, here]
        arrived(y_in_flight)
        packed = mm(pack, yrecv[a]).astype(BF)
        for g in range(groups):
            for ch in range(CHUNKS):
                first = g * per_z + starts[ch]
                zsend[(a * CHUNKS + ch) * groups + g, : PARTS[ch]] = packed[
                    first : first + PARTS[ch]
                ]

    place = z % HSPLIT

    def z_device(other, to):
        group = 1 - zgroup if other else zgroup
        return (dp, y * nz + group * HSPLIT + to)

    def z_rows(n, ch, source):
        return block(rows, source, PARTS[ch], n)

    def z_source(tag):
        group = 1 - zgroup if tag >= HSPLIT else zgroup
        return group * HSPLIT + tag % HSPLIT

    def z_first(n, ch, at, j):
        other, to = Z_FIRST[at][j]
        group = 1 - zgroup if other else zgroup
        tag = at + HSPLIT * other
        return remote(
            zsend.at[n * groups + group, pl.ds(0, PARTS[ch])],
            z_rows(n, ch, z),
            z_ss.at[n, j],
            z_rs.at[n, tag],
            z_device(other, to),
        )

    def z_second(n, ch, at, j):
        tag, to = Z_SECOND[at][j]
        view = z_rows(n, ch, z_source(tag))
        return remote(view, view, z_ss.at[n, 4 + j], z_rs.at[n, tag], z_device(False, to))

    def z_arrival(n, ch, tag):
        view = z_rows(n, ch, z_source(tag))
        remote(view, view, z_ss.at[n, 0], z_rs.at[n, tag], sibling).wait_recv()

    def each_place(step):
        for at in range(HSPLIT):
            pl.when(place == at)(functools.partial(step, at))

    def z_start(a, ch):
        n = a * CHUNKS + ch
        part = PARTS[ch]

        def step(at):
            for j in range(len(Z_FIRST[at])):
                z_first(n, ch, at, j).start()

        each_place(step)
        rows[n, pl.ds(pl.multiple_of(z * part, 16), part)] = zsend[n * groups + zgroup, :part]

    def z_pass(a, ch):
        n = a * CHUNKS + ch

        def step(at):
            done = []
            for j, (tag, _) in enumerate(Z_SECOND[at]):
                if tag not in done:
                    z_arrival(n, ch, tag)
                    done.append(tag)
                z_second(n, ch, at, j).start()

        each_place(step)

    def z_finish(a, ch):
        n = a * CHUNKS + ch

        def step(at):
            passed = [tag for tag, _ in Z_SECOND[at]]
            for tag in range(nz):
                if tag != at and tag not in passed:
                    z_arrival(n, ch, tag)

        each_place(step)

    def z_sent(n, ch):
        def step(at):
            for j in range(len(Z_FIRST[at])):
                z_first(n, ch, at, j).wait_send()
            for j in range(len(Z_SECOND[at])):
                z_second(n, ch, at, j).wait_send()

        each_place(step)

    def product(a, ch, w, mine):
        start = pl.multiple_of((core if mine else 1 - core) * half, 128)
        return mm(rows[a * CHUNKS + ch, : nz * PARTS[ch]], w[:, pl.ds(start, half)])

    def cores_send(p, ch, a, w):
        n = p * CHUNKS + ch
        total = nz * PARTS[ch]
        csend[n, :total] = product(a, ch, w, False).astype(BF)
        at = pl.ds(0, total)
        copy = remote(csend.at[n, at], crecv.at[n, at], c_ss.at[n], c_rs.at[n], sibling)
        copy.start()
        return copy

    def shard_at(ch, k):
        shard = nz * PARTS[ch] // nx
        return pl.ds(pl.multiple_of((x + nx + k) % nx * shard, 16), shard)

    def x_copy(n, ch, role, source, k):
        where = pl.ds(0, nz * PARTS[ch] // nx)
        return remote(
            source, rrecv.at[n, role, where], r_ss.at[n, role], r_rs.at[n, role], at_x(k + nx)[1]
        )

    def x_scatter(p, ch, a, w, core_copy):
        n = p * CHUNKS + ch
        total = nz * PARTS[ch]
        value = product(a, ch, w, True)
        core_copy.wait_recv()
        value = value + crecv[n, :total].astype(F32)
        own[n, :total] = value
        rsend[n, :total] = value.astype(BF)
        copies = {}
        if nx > 1:
            far = 2 if (p + ch) % 2 == 0 else -2
            for role, shard, k in ((4, 4, far), (2, 3, 1), (3, -3, -1), (0, 1, 1), (1, -1, -1)):
                copies[role] = x_copy(n, ch, role, rsend.at[n, shard_at(ch, shard)], k)
                copies[role].start()
        return copies

    def x_combine(p, ch, copies):
        n = p * CHUNKS + ch
        shard = nz * PARTS[ch] // nx
        if nx > 1:
            even = (p + ch) % 2 == 0
            copies[2].wait_recv()
            copies[3].wait_recv()
            copies[4].wait_recv()
            for i, k in ((0, 2), (1, -2)) if even else ((1, -2), (0, 2)):
                value = own[n, shard_at(ch, k)] + rrecv[n, 2 + i, :shard].astype(F32)
                if even == (i == 0):
                    value = value + rrecv[n, 4, :shard].astype(F32)
                xcomb[n, i, :shard] = value.astype(BF)
                copies[5 + i] = x_copy(n, ch, 5 + i, xcomb.at[n, i, pl.ds(0, shard)], k)
                copies[5 + i].start()

    def x_sum(p, ch, copies):
        n = p * CHUNKS + ch
        shard = nz * PARTS[ch] // nx
        value = own[n, shard_at(ch, 0)]
        for role in (0, 1, 5, 6) if nx > 1 else ():
            copies[role].wait_recv()
            value = value + rrecv[n, role, :shard].astype(F32)
        return value

    def act_view(a, ch, k):
        return acts.at[(a * CHUNKS + ch) * CORES + core, shard_at(ch, k)]

    def to_sibling(a, ch, k):
        n = a * CHUNKS + ch
        view = act_view(a, ch, -k)
        copy = remote(view, view, s_ss.at[n, k], s_rs.at[n, k], sibling)
        copy.start()
        return copy

    def gather_copy(a, ch, k, away, target):
        n = a * CHUNKS + ch
        view = act_view(a, ch, away)
        return remote(view, view, a_ss.at[n, k], a_rs.at[n, k], at_x(target + nx)[1])

    def activate(ch, scatters):
        gate_pre = x_sum(0, ch, scatters[0])
        up_pre = x_sum(1, ch, scatters[1])
        sigma = 1.0 / (1.0 + jnp.exp(-gate_pre))
        gate_factor = up_pre * sigma * (1.0 + gate_pre * (1.0 - sigma))
        up_factor = gate_pre * sigma
        hidden_grad = x_sum(2, ch, scatters[2])
        mine = shard_at(ch, 0)
        acts[ch * CORES + core, mine] = (hidden_grad * gate_factor).astype(BF)
        acts[(CHUNKS + ch) * CORES + core, mine] = (hidden_grad * up_factor).astype(BF)
        gathers = {}
        if nx > 1:
            for k in (2, nx - 2, 1, nx - 1):
                for a in range(2):
                    gathers[a, k] = gather_copy(a, ch, k, 0, k)
                    gathers[a, k].start()
        forwards = [to_sibling(a, ch, 0) for a in range(2)]
        return gathers, forwards

    def pass_on(ch, gathers, forwards):
        if nx == 1:
            return
        for k in (2, nx - 2):
            step = 1 if k == 2 else -1
            for a in range(2):
                gathers[a, k].wait_recv()
                if (a == 0) == (k == 2):
                    gathers[a, 4] = gather_copy(a, ch, 4, -2 * step, 2 * step)
                    gathers[a, 4].start()
                third = 3 if k == 2 else nx - 3
                gathers[a, third] = gather_copy(a, ch, third, -2 * step, step)
                gathers[a, third].start()
                forwards.append(to_sibling(a, ch, k))

    def pass_rest(ch, gathers, forwards):
        if nx == 1:
            return
        for k in (1, nx - 1, 3, nx - 3, 4):
            for a in range(2):
                gathers[a, k].wait_recv()
                forwards.append(to_sibling(a, ch, k))

    def give_back(ch, forwards):
        part = PARTS[ch]
        total = nz * part
        for copy in forwards:
            copy.wait_recv()
        value = None
        for a, w in ((0, w_gate), (1, w_up)):
            for c in range(CORES):
                act = acts[(a * CHUNKS + ch) * CORES + c, :total]
                term = mm_nt(act, w[:, c * half : (c + 1) * half])
                value = term if value is None else value + term
        back[ch, :total] = value.astype(BF)

        def step(at):
            for j, (tag, other, to, buffer) in enumerate(back_sends(at)):
                b_copy(ch, block(back, z_source(tag), part, ch), j, buffer, other, to).start()

        each_place(step)

    def b_copy(ch, source, j, buffer, other, to):
        where = zret.at[ch, buffer, pl.ds(0, PARTS[ch])]
        return remote(source, where, b_ss.at[ch, j], b_rs.at[ch, buffer], z_device(other, to))

    def b_arrival(ch, buffer):
        b_copy(ch, zcomb.at[ch, 0, pl.ds(0, PARTS[ch])], 0, buffer, False, 0).wait_recv()

    def back_block(ch, source):
        part = PARTS[ch]
        return back[ch, pl.ds(pl.multiple_of(source * part, 16), part)].astype(F32)

    def pass_back(ch):
        part = PARTS[ch]

        def step(at):
            first = len(back_sends(at))
            for i, (tag, parts, other, to, buffer) in enumerate(back_relays(at)):
                value = back_block(ch, z_source(tag))
                for j in parts:
                    b_arrival(ch, 4 + j)
                    value = value + zret[ch, 4 + j, :part].astype(F32)
                zcomb[ch, i, :part] = value.astype(BF)
                source = zcomb.at[ch, i, pl.ds(0, part)]
                b_copy(ch, source, first + i, buffer, other, to).start()

        each_place(step)

    def add_back(ch):
        part = PARTS[ch]

        def step(at):
            sums = [back_block(ch, z), None]
            for j, (other, _) in enumerate(Z_FIRST[at]):
                b_arrival(ch, j)
                term = zret[ch, j, :part].astype(F32)
                sums[other] = term if sums[other] is None else sums[other] + term
            zsum[ch * groups + zgroup, :part] = sums[0].astype(BF)
            zsum[ch * groups + 1 - zgroup, :part] = sums[1].astype(BF)

        each_place(step)

    def back_sent(ch):
        def step(at):
            for j in range(len(back_sends(at)) + len(back_relays(at))):
                b_copy(ch, zcomb.at[ch, 0, pl.ds(0, PARTS[ch])], j, 0, False, 0).wait_send()

        each_place(step)

    starts = [sum(PARTS[:ch]) for ch in range(CHUNKS)]
    weights = ((0, w_gate), (0, w_up), (1, w_down_t))

    pack_rows(0, y_in)
    z_start(0, 0)
    pack_rows(1, y_gr)
    z_start(1, 0)
    z_pass(0, 0)
    for name in ("w_gate", "w_up", "w_down"):
        loads[name].wait()
    cores = []
    scatters = [[] for _ in PARTS]
    gathers = [None] * CHUNKS
    forwards = [None] * CHUNKS

    def scatter_forward(ch):
        if ch + 1 < CHUNKS:
            z_start(0, ch + 1)
        z_finish(0, ch)
        pair = [cores_send(p, ch, *weights[p]) for p in (0, 1)]
        z_pass(1, ch)
        if ch + 1 < CHUNKS:
            z_start(1, ch + 1)
        for p in (0, 1):
            scatters[ch].append(x_scatter(p, ch, *weights[p], pair[p]))
        cores.extend(pair)

    def scatter_down(ch):
        z_finish(1, ch)
        copy = cores_send(2, ch, *weights[2])
        if ch + 1 < CHUNKS:
            z_pass(0, ch + 1)
        x_combine(0, ch, scatters[ch][0])
        x_combine(1, ch, scatters[ch][1])
        scatters[ch].append(x_scatter(2, ch, *weights[2], copy))
        cores.append(copy)

    def gather(ch):
        gathers[ch], forwards[ch] = activate(ch, scatters[ch])

    for ch in range(CHUNKS):
        scatter_forward(ch)
        if ch > 0:
            gather(ch - 1)
        scatter_down(ch)
        if ch > 0:
            pass_on(ch - 1, gathers[ch - 1], forwards[ch - 1])
        x_combine(2, ch, scatters[ch][2])
        if ch > 0:
            pass_rest(ch - 1, gathers[ch - 1], forwards[ch - 1])
            give_back(ch - 1, forwards[ch - 1])
    last = CHUNKS - 1
    gather(last)
    for ch in range(last):
        pass_back(ch)
    pass_on(last, gathers[last], forwards[last])
    pass_rest(last, gathers[last], forwards[last])
    give_back(last, forwards[last])

    for a, grad in ((0, grad_gate), (1, grad_up)):
        for c in range(CORES):
            value = None
            for ch in range(CHUNKS):
                total = nz * PARTS[ch]
                term = mm_tn(rows[ch, :total], acts[(a * CHUNKS + ch) * CORES + c, :total])
                value = term if value is None else value + term
            grad[:, c * half : (c + 1) * half] = value.astype(BF)

    stores = []
    for source, target in ((grad_gate, grad_gate_h), (grad_up, grad_up_h)):
        stores.append(pltpu.make_async_copy(source, target, l_s.at[len(loads) + len(stores)]))
        stores[-1].start()
    y_back = {}
    for k in near_first(ny):
        t, device = at_y(k)
        y_back[k] = remote(block(yback, t, blk), block(yret, y, blk), e_ss.at[k], e_rs.at[k], device)

    for ch in range(CHUNKS):
        if ch == last:
            pass_back(ch)
        add_back(ch)
        part = PARTS[ch]
        spread = None
        for g in range(groups):
            first = g * per_z + starts[ch]
            term = mm(unpack[:, first : first + part], zsum[ch * groups + g, :part])
            spread = term if spread is None else spread + term
        spread = spread.astype(BF)
        for t in range(ch, ny, CHUNKS):
            yback[t * blk : (t + 1) * blk] = spread[t * blk : (t + 1) * blk]

        def step(parity):
            for k in near_first(ny):
                if (k + parity) % 2 == ch:
                    y_back[k].start()

        for parity in range(2):
            pl.when(y % 2 == parity)(functools.partial(step, parity))
    here = pl.ds(pl.multiple_of(y * blk, 16), blk)
    yret[here] = yback[here]
    arrived(y_back)
    in_grad_t[...] = mm_tn(yret[...], pick[...]).astype(BF)
    stores.append(pltpu.make_async_copy(in_grad_t, in_grad_h, l_s.at[len(loads) + len(stores)]))
    stores[-1].start()

    for a in range(2):
        for ch in range(CHUNKS):
            z_sent(a * CHUNKS + ch, ch)
    for copy in stores:
        copy.wait()
    for ch in range(CHUNKS):
        back_sent(ch)
    flat = [y_in, y_gr, y_back, *gathers]
    for each in scatters:
        flat.extend(each)
    for copies in flat:
        for copy in copies.values():
            copy.wait_send()
    for copy in cores:
        copy.wait_send()
    for each in forwards:
        for copy in each:
            copy.wait_send()


def per_device(sizes, out_grad, inputs, expert_ids, gate_weights, w_gate, w_up, w_down):
    nx, ny, nz = sizes
    tokens, feature = out_grad.shape
    hidden = w_gate.shape[1]
    half = hidden // CORES
    groups = nz // HSPLIT
    slots = ny * groups * SLOT
    per_z = ny * CAP
    part = max(PARTS)
    total = nz * part
    shard = total // nx
    dma = pltpu.SemaphoreType.DMA
    vmem = pltpu.VMEM
    in_grad_t, grad_gate, grad_up = pl.pallas_call(
        functools.partial(kernel, sizes),
        out_shape=(
            jax.ShapeDtypeStruct((feature, tokens), BF),
            jax.ShapeDtypeStruct((feature, hidden), BF),
            jax.ShapeDtypeStruct((feature, hidden), BF),
        ),
        in_specs=[pl.BlockSpec(memory_space=pltpu.HBM)] * 7,
        out_specs=(pl.BlockSpec(memory_space=pltpu.HBM),) * 3,
        scratch_shapes=[
            vmem((feature, tokens), BF),
            vmem((feature, hidden), BF),
            vmem((feature, hidden), BF),
            vmem((feature, tokens), BF),
            vmem((feature, tokens), BF),
            vmem((expert_ids.shape[1], tokens), jnp.int32),
            vmem((expert_ids.shape[1], tokens), F32),
            vmem((feature, hidden), BF),
            vmem((feature, hidden), BF),
            vmem((feature, hidden), BF),
            vmem((slots, tokens), BF),
            vmem((2, slots, feature), BF),
            vmem((2, slots, feature), BF),
            vmem((2 * CHUNKS * groups, part, feature), BF),
            vmem((2 * CHUNKS, total, feature), BF),
            vmem((3 * CHUNKS, total, half), BF),
            vmem((3 * CHUNKS, total, half), BF),
            vmem((3 * CHUNKS, total, half), F32),
            vmem((3 * CHUNKS, total, half), BF),
            vmem((3 * CHUNKS, 7, shard, half), BF),
            vmem((3 * CHUNKS, 2, shard, half), BF),
            vmem((2 * CHUNKS * CORES, total, half), BF),
            vmem((CHUNKS, total, feature), BF),
            vmem((CHUNKS, 8, part, feature), BF),
            vmem((CHUNKS, 3, part, feature), BF),
            vmem((CHUNKS * groups, part, feature), BF),
            vmem((slots, feature), BF),
            vmem((slots, feature), BF),
            dma((2, ny)),
            dma((2, ny)),
            dma((2 * CHUNKS, 8)),
            dma((2 * CHUNKS, nz)),
            dma((3 * CHUNKS,)),
            dma((3 * CHUNKS,)),
            dma((3 * CHUNKS, 7)),
            dma((3 * CHUNKS, 7)),
            dma((2 * CHUNKS, nx)),
            dma((2 * CHUNKS, nx)),
            dma((2 * CHUNKS, nx)),
            dma((2 * CHUNKS, nx)),
            dma((CHUNKS, 8)),
            dma((CHUNKS, 8)),
            dma((ny,)),
            dma((ny,)),
            dma((10,)),
        ],
        compiler_params=pltpu.CompilerParams(
            collective_id=0, has_side_effects=True, vmem_limit_bytes=56 * 1024 * 1024
        ),
        cost_estimate=pl.CostEstimate(
            flops=14 * nz * per_z * feature * hidden, bytes_accessed=4_000_000, transcendentals=0
        ),
    )(out_grad.T, inputs.T, expert_ids.T, gate_weights.T, w_gate, w_up, w_down.T)
    return in_grad_t.T, grad_gate, grad_up


def solution(mesh, sizes=None):
    if sizes is None:
        ny, nz = grid_of(mesh.shape["expert"])
        sizes = (mesh.shape["dp"] // CORES, ny, nz)
    placed = (
        P("expert", "dp"),
        P("expert", "dp"),
        P("expert", None),
        P("expert", None),
        P("dp", "expert"),
        P("dp", "expert"),
        P("expert", "dp"),
    )
    return jax.shard_map(
        functools.partial(per_device, sizes),
        mesh=mesh,
        in_specs=placed,
        out_specs=(P("expert", "dp"), P("dp", "expert"), P("dp", "expert")),
        check_vma=False,
    )
```

```python
import functools

import jax
import jax.numpy as jnp
from jax import lax
from jax.experimental import pallas as pl
from jax.experimental.pallas import tpu as pltpu
from jax.sharding import PartitionSpec as P

HSPLIT = 4
CAP = 12
SLOT = 16
PARTS = (48, 48)
CHUNKS = len(PARTS)
Z_FIRST = (
    ((0, 1), (1, 1), (1, 3)),
    ((0, 2), (1, 3), (1, 0), (0, 0)),
    ((0, 1), (1, 0), (1, 3), (0, 3)),
    ((0, 2), (1, 2), (1, 0)),
)
Z_SECOND = (
    ((7, 1), (6, 1), (5, 1)),
    ((0, 3), (0, 2), (4, 0), (2, 0)),
    ((3, 0), (3, 1), (7, 3), (1, 3)),
    ((4, 2), (5, 2), (6, 2)),
)
CORES = 2
BF = jnp.bfloat16
F32 = jnp.float32


def relay_tags(at):
    return list(dict.fromkeys(tag for tag, _ in Z_SECOND[at]))


def back_sends(at):
    plan = []
    for relay in range(HSPLIT):
        for j, (tag, to) in enumerate(Z_SECOND[relay]):
            if to == at:
                plan.append((tag, False, relay, 4 + j))
    for home in range(HSPLIT):
        for j, (other, to) in enumerate(Z_FIRST[home]):
            tag = home + HSPLIT * other
            if to == at and tag not in relay_tags(at):
                plan.append((tag, other == 1, home, j))
    return plan


def back_relays(at):
    plan = []
    for tag in relay_tags(at):
        parts = [j for j, (each, _) in enumerate(Z_SECOND[at]) if each == tag]
        home, other = tag % HSPLIT, tag // HSPLIT
        plan.append((tag, parts, other == 1, home, Z_FIRST[home].index((other, at))))
    return plan


def grid_of(devices):
    side = 1
    while side * side < devices:
        side *= 2
    return devices // side, side


def mm(a, b):
    return lax.dot_general(a, b, (((1,), (0,)), ((), ())), preferred_element_type=F32)


def mm_nt(a, b):
    return lax.dot_general(a, b, (((1,), (1,)), ((), ())), preferred_element_type=F32)


def mm_tn(a, b):
    return lax.dot_general(a, b, (((0,), (0,)), ((), ())), preferred_element_type=F32)


def iota(shape, dim):
    return lax.broadcasted_iota(jnp.int32, shape, dim)


def near_first(n):
    order = []
    for k in range(1, n // 2 + 1):
        order.append(k)
        if n - k != k:
            order.append(n - k)
    return order


def kernel(
    sizes,
    out_grad_h,
    inputs_h,
    ids_h,
    gates_h,
    w_gate_h,
    w_up_h,
    w_down_h,
    in_grad_h,
    grad_gate_h,
    grad_up_h,
    in_grad_t,
    grad_gate,
    grad_up,
    out_grad_t,
    inputs_t,
    ids_t,
    gates_t,
    w_gate,
    w_up,
    w_down_t,
    pick,
    ysend,
    yrecv,
    zsend,
    rows,
    csend,
    crecv,
    own,
    rsend,
    rrecv,
    xcomb,
    acts,
    back,
    zret,
    zcomb,
    zsum,
    yback,
    yret,
    y_ss,
    y_rs,
    z_ss,
    z_rs,
    c_ss,
    c_rs,
    r_ss,
    r_rs,
    a_ss,
    a_rs,
    s_ss,
    s_rs,
    b_ss,
    b_rs,
    e_ss,
    e_rs,
    l_s,
):
    nx, ny, nz = sizes
    groups = nz // HSPLIT
    blk = groups * SLOT
    slots = ny * blk
    per_z = ny * CAP
    tokens = ids_t.shape[1]
    half = w_gate.shape[1] // CORES

    dp = lax.axis_index("dp")
    ex = lax.axis_index("expert")
    x, core = dp // CORES, dp % CORES
    y, z = ex // nz, ex % nz
    zgroup = z // HSPLIT
    sibling = (x * CORES + 1 - core, ex)

    def at_y(k):
        t = (y + k) % ny
        return t, (dp, t * nz + z)

    def at_z(k):
        t = (z + k) % nz
        return t, (dp, y * nz + t)

    def at_x(k):
        t = (x + k) % nx
        return t, (t * CORES + core, ex)

    def remote(src, dst, ssem, rsem, device):
        return pltpu.make_async_remote_copy(
            src_ref=src,
            dst_ref=dst,
            send_sem=ssem,
            recv_sem=rsem,
            device_id=device,
            device_id_type=pl.DeviceIdType.MESH,
        )

    loads = {}
    for name, (source, target) in dict(
        ids=(ids_h, ids_t),
        inputs=(inputs_h, inputs_t),
        gates=(gates_h, gates_t),
        out_grad=(out_grad_h, out_grad_t),
        w_gate=(w_gate_h, w_gate),
        w_up=(w_up_h, w_up),
        w_down=(w_down_h, w_down_t),
    ).items():
        loads[name] = pltpu.make_async_copy(source, target, l_s.at[len(loads)])
        loads[name].start()

    partners = (
        [at_y(k)[1] for k in range(1, ny)]
        + [at_z(k)[1] for k in range(1, nz)]
        + [at_x(k)[1] for k in range(1, nx)]
        + [sibling]
    )
    barrier = pltpu.get_barrier_semaphore()
    for device in partners:
        pl.semaphore_signal(barrier, inc=1, device_id=device, device_id_type=pl.DeviceIdType.MESH)

    expert = iota((128, tokens), 0)
    hits = jnp.zeros((128, tokens), F32)
    loads["ids"].wait()
    loads["gates"].wait()
    gate = jnp.zeros((128, tokens), F32)
    for k in range(ids_t.shape[0]):
        hit = ids_t[k : k + 1, :] == expert
        hits = hits + jnp.where(hit, 1.0, 0.0)
        gate = gate + jnp.where(hit, gates_t[k : k + 1, :], 0.0)
    hits_b = hits.astype(BF)
    before = jnp.where(iota((tokens, tokens), 0) < iota((tokens, tokens), 1), 1.0, 0.0).astype(BF)
    slot_of = mm(hits_b, before).astype(BF)
    expand = jnp.where(iota((slots, 128), 0) // SLOT == iota((slots, 128), 1), 1.0, 0.0).astype(BF)
    hit_rt = mm(expand, hits_b)
    slot_rt = mm(expand, slot_of)
    wanted = (iota((slots, tokens), 0) % SLOT).astype(F32)
    picker = jnp.where(jnp.logical_and(hit_rt > 0.5, slot_rt == wanted), 1.0, 0.0)
    picker_b = picker.astype(BF)
    pick[...] = picker_b

    def block(ref, index, count, *lead):
        return ref.at[(*lead, pl.ds(pl.multiple_of(index * count, 16), count))]

    def y_copies(a):
        copies = {}
        for k in near_first(ny):
            t, device = at_y(k)
            copies[k] = remote(
                block(ysend, t, blk, a),
                block(yrecv, y, blk, a),
                y_ss.at[a, k],
                y_rs.at[a, k],
                device,
            )
            copies[k].start()
        return copies

    loads["inputs"].wait()
    ysend[0] = mm_nt(picker_b, inputs_t[...]).astype(BF)
    pl.semaphore_wait(barrier, len(partners))
    y_in = y_copies(0)
    gate_1 = gate.astype(BF)
    rest = gate - gate_1.astype(F32)
    gate_2 = rest.astype(BF)
    gate_3 = (rest - gate_2.astype(F32)).astype(BF)
    gate_rt = mm(expand, gate_1) + mm(expand, gate_2) + mm(expand, gate_3)
    scale = jnp.sum(picker * gate_rt, axis=1, keepdims=True)
    loads["out_grad"].wait()
    ysend[1] = (scale * mm_nt(picker_b, out_grad_t[...])).astype(BF)
    y_gr = y_copies(1)

    def turn(value):
        return value % 2 * (ny // 2) + value // 2

    col = iota((groups * per_z, slots), 1)
    seat = (col // SLOT % groups) * per_z + turn(col // blk) * CAP + col % SLOT
    pack = jnp.where(
        jnp.logical_and(seat == iota((groups * per_z, slots), 0), col % SLOT < CAP), 1.0, 0.0
    ).astype(BF)
    row = iota((slots, groups * per_z), 0)
    seat_t = (row // SLOT % groups) * per_z + turn(row // blk) * CAP + row % SLOT
    unpack = jnp.where(
        jnp.logical_and(seat_t == iota((slots, groups * per_z), 1), row % SLOT < CAP), 1.0, 0.0
    ).astype(BF)

    def arrived(copies):
        for copy in copies.values():
            copy.wait_recv()

    def pack_rows(a, y_in_flight):
        here = pl.ds(pl.multiple_of(y * blk, 16), blk)
        yrecv[a, here] = ysend[a, here]
        arrived(y_in_flight)
        packed = mm(pack, yrecv[a]).astype(BF)
        for g in range(groups):
            for ch in range(CHUNKS):
                first = g * per_z + starts[ch]
                zsend[(a * CHUNKS + ch) * groups + g, : PARTS[ch]] = packed[
                    first : first + PARTS[ch]
                ]

    place = z % HSPLIT

    def z_device(other, to):
        group = 1 - zgroup if other else zgroup
        return (dp, y * nz + group * HSPLIT + to)

    def z_rows(n, ch, source):
        return block(rows, source, PARTS[ch], n)

    def z_source(tag):
        group = 1 - zgroup if tag >= HSPLIT else zgroup
        return group * HSPLIT + tag % HSPLIT

    def z_first(n, ch, at, j):
        other, to = Z_FIRST[at][j]
        group = 1 - zgroup if other else zgroup
        tag = at + HSPLIT * other
        return remote(
            zsend.at[n * groups + group, pl.ds(0, PARTS[ch])],
            z_rows(n, ch, z),
            z_ss.at[n, j],
            z_rs.at[n, tag],
            z_device(other, to),
        )

    def z_second(n, ch, at, j):
        tag, to = Z_SECOND[at][j]
        view = z_rows(n, ch, z_source(tag))
        return remote(view, view, z_ss.at[n, 4 + j], z_rs.at[n, tag], z_device(False, to))

    def z_arrival(n, ch, tag):
        view = z_rows(n, ch, z_source(tag))
        remote(view, view, z_ss.at[n, 0], z_rs.at[n, tag], sibling).wait_recv()

    def each_place(step):
        for at in range(HSPLIT):
            pl.when(place == at)(functools.partial(step, at))

    def z_start(a, ch):
        n = a * CHUNKS + ch
        part = PARTS[ch]

        def step(at):
            for j in range(len(Z_FIRST[at])):
                z_first(n, ch, at, j).start()

        each_place(step)
        rows[n, pl.ds(pl.multiple_of(z * part, 16), part)] = zsend[n * groups + zgroup, :part]

    def z_pass(a, ch):
        n = a * CHUNKS + ch

        def step(at):
            done = []
            for j, (tag, _) in enumerate(Z_SECOND[at]):
                if tag not in done:
                    z_arrival(n, ch, tag)
                    done.append(tag)
                z_second(n, ch, at, j).start()

        each_place(step)

    def z_finish(a, ch):
        n = a * CHUNKS + ch

        def step(at):
            passed = [tag for tag, _ in Z_SECOND[at]]
            for tag in range(nz):
                if tag != at and tag not in passed:
                    z_arrival(n, ch, tag)

        each_place(step)

    def z_sent(n, ch):
        def step(at):
            for j in range(len(Z_FIRST[at])):
                z_first(n, ch, at, j).wait_send()
            for j in range(len(Z_SECOND[at])):
                z_second(n, ch, at, j).wait_send()

        each_place(step)

    def product(a, ch, w, mine):
        start = pl.multiple_of((core if mine else 1 - core) * half, 128)
        return mm(rows[a * CHUNKS + ch, : nz * PARTS[ch]], w[:, pl.ds(start, half)])

    def cores_send(p, ch, a, w):
        n = p * CHUNKS + ch
        total = nz * PARTS[ch]
        csend[n, :total] = product(a, ch, w, False).astype(BF)
        at = pl.ds(0, total)
        copy = remote(csend.at[n, at], crecv.at[n, at], c_ss.at[n], c_rs.at[n], sibling)
        copy.start()
        return copy

    def shard_at(ch, k):
        shard = nz * PARTS[ch] // nx
        return pl.ds(pl.multiple_of((x + nx + k) % nx * shard, 16), shard)

    def x_copy(n, ch, role, source, k):
        where = pl.ds(0, nz * PARTS[ch] // nx)
        return remote(
            source, rrecv.at[n, role, where], r_ss.at[n, role], r_rs.at[n, role], at_x(k + nx)[1]
        )

    def x_scatter(p, ch, a, w, core_copy):
        n = p * CHUNKS + ch
        total = nz * PARTS[ch]
        value = product(a, ch, w, True)
        core_copy.wait_recv()
        value = value + crecv[n, :total].astype(F32)
        own[n, :total] = value
        rsend[n, :total] = value.astype(BF)
        copies = {}
        if nx > 1:
            far = 2 if (p + ch) % 2 == 0 else -2
            for role, shard, k in ((4, 4, far), (2, 3, 1), (3, -3, -1), (0, 1, 1), (1, -1, -1)):
                copies[role] = x_copy(n, ch, role, rsend.at[n, shard_at(ch, shard)], k)
                copies[role].start()
        return copies

    def x_combine(p, ch, copies):
        n = p * CHUNKS + ch
        shard = nz * PARTS[ch] // nx
        if nx > 1:
            even = (p + ch) % 2 == 0
            copies[2].wait_recv()
            copies[3].wait_recv()
            copies[4].wait_recv()
            for i, k in ((0, 2), (1, -2)) if even else ((1, -2), (0, 2)):
                value = own[n, shard_at(ch, k)] + rrecv[n, 2 + i, :shard].astype(F32)
                if even == (i == 0):
                    value = value + rrecv[n, 4, :shard].astype(F32)
                xcomb[n, i, :shard] = value.astype(BF)
                copies[5 + i] = x_copy(n, ch, 5 + i, xcomb.at[n, i, pl.ds(0, shard)], k)
                copies[5 + i].start()

    def x_sum(p, ch, copies):
        n = p * CHUNKS + ch
        shard = nz * PARTS[ch] // nx
        value = own[n, shard_at(ch, 0)]
        for role in (0, 1, 5, 6) if nx > 1 else ():
            copies[role].wait_recv()
            value = value + rrecv[n, role, :shard].astype(F32)
        return value

    def act_view(a, ch, k):
        return acts.at[(a * CHUNKS + ch) * CORES + core, shard_at(ch, k)]

    def to_sibling(a, ch, k):
        n = a * CHUNKS + ch
        view = act_view(a, ch, -k)
        copy = remote(view, view, s_ss.at[n, k], s_rs.at[n, k], sibling)
        copy.start()
        return copy

    def gather_copy(a, ch, k, away, target):
        n = a * CHUNKS + ch
        view = act_view(a, ch, away)
        return remote(view, view, a_ss.at[n, k], a_rs.at[n, k], at_x(target + nx)[1])

    def activate(ch, scatters):
        gate_pre = x_sum(0, ch, scatters[0])
        up_pre = x_sum(1, ch, scatters[1])
        sigma = 1.0 / (1.0 + jnp.exp(-gate_pre))
        gate_factor = up_pre * sigma * (1.0 + gate_pre * (1.0 - sigma))
        up_factor = gate_pre * sigma
        hidden_grad = x_sum(2, ch, scatters[2])
        mine = shard_at(ch, 0)
        acts[ch * CORES + core, mine] = (hidden_grad * gate_factor).astype(BF)
        acts[(CHUNKS + ch) * CORES + core, mine] = (hidden_grad * up_factor).astype(BF)
        gathers = {}
        if nx > 1:
            for k in (2, nx - 2, 1, nx - 1):
                for a in range(2):
                    gathers[a, k] = gather_copy(a, ch, k, 0, k)
                    gathers[a, k].start()
        forwards = [to_sibling(a, ch, 0) for a in range(2)]
        return gathers, forwards

    def pass_on(ch, gathers, forwards):
        if nx == 1:
            return
        for k in (2, nx - 2):
            step = 1 if k == 2 else -1
            for a in range(2):
                gathers[a, k].wait_recv()
                if (a == 0) == (k == 2):
                    gathers[a, 4] = gather_copy(a, ch, 4, -2 * step, 2 * step)
                    gathers[a, 4].start()
                third = 3 if k == 2 else nx - 3
                gathers[a, third] = gather_copy(a, ch, third, -2 * step, step)
                gathers[a, third].start()
                forwards.append(to_sibling(a, ch, k))

    def pass_rest(ch, gathers, forwards):
        if nx == 1:
            return
        for k in (1, nx - 1, 3, nx - 3, 4):
            for a in range(2):
                gathers[a, k].wait_recv()
                forwards.append(to_sibling(a, ch, k))

    def give_back(ch, forwards):
        part = PARTS[ch]
        total = nz * part
        for copy in forwards:
            copy.wait_recv()
        value = None
        for a, w in ((0, w_gate), (1, w_up)):
            for c in range(CORES):
                act = acts[(a * CHUNKS + ch) * CORES + c, :total]
                term = mm_nt(act, w[:, c * half : (c + 1) * half])
                value = term if value is None else value + term
        back[ch, :total] = value.astype(BF)

        def step(at):
            for j, (tag, other, to, buffer) in enumerate(back_sends(at)):
                b_copy(ch, block(back, z_source(tag), part, ch), j, buffer, other, to).start()

        each_place(step)

    def b_copy(ch, source, j, buffer, other, to):
        where = zret.at[ch, buffer, pl.ds(0, PARTS[ch])]
        return remote(source, where, b_ss.at[ch, j], b_rs.at[ch, buffer], z_device(other, to))

    def b_arrival(ch, buffer):
        b_copy(ch, zcomb.at[ch, 0, pl.ds(0, PARTS[ch])], 0, buffer, False, 0).wait_recv()

    def back_block(ch, source):
        part = PARTS[ch]
        return back[ch, pl.ds(pl.multiple_of(source * part, 16), part)].astype(F32)

    def pass_back(ch):
        part = PARTS[ch]

        def step(at):
            first = len(back_sends(at))
            for i, (tag, parts, other, to, buffer) in enumerate(back_relays(at)):
                value = back_block(ch, z_source(tag))
                for j in parts:
                    b_arrival(ch, 4 + j)
                    value = value + zret[ch, 4 + j, :part].astype(F32)
                zcomb[ch, i, :part] = value.astype(BF)
                source = zcomb.at[ch, i, pl.ds(0, part)]
                b_copy(ch, source, first + i, buffer, other, to).start()

        each_place(step)

    def add_back(ch):
        part = PARTS[ch]

        def step(at):
            sums = [back_block(ch, z), None]
            for j, (other, _) in enumerate(Z_FIRST[at]):
                b_arrival(ch, j)
                term = zret[ch, j, :part].astype(F32)
                sums[other] = term if sums[other] is None else sums[other] + term
            zsum[ch * groups + zgroup, :part] = sums[0].astype(BF)
            zsum[ch * groups + 1 - zgroup, :part] = sums[1].astype(BF)

        each_place(step)

    def back_sent(ch):
        def step(at):
            for j in range(len(back_sends(at)) + len(back_relays(at))):
                b_copy(ch, zcomb.at[ch, 0, pl.ds(0, PARTS[ch])], j, 0, False, 0).wait_send()

        each_place(step)

    starts = [sum(PARTS[:ch]) for ch in range(CHUNKS)]
    weights = ((0, w_gate), (0, w_up), (1, w_down_t))

    pack_rows(0, y_in)
    z_start(0, 0)
    pack_rows(1, y_gr)
    z_start(1, 0)
    z_pass(0, 0)
    for name in ("w_gate", "w_up", "w_down"):
        loads[name].wait()
    cores = []
    scatters = [[] for _ in PARTS]
    gathers = [None] * CHUNKS
    forwards = [None] * CHUNKS

    def scatter_forward(ch):
        if ch + 1 < CHUNKS:
            z_start(0, ch + 1)
        else:
            z_pass(1, ch)
        z_finish(0, ch)
        pair = [cores_send(p, ch, *weights[p]) for p in (0, 1)]
        if ch + 1 < CHUNKS:
            z_pass(1, ch)
            z_start(1, ch + 1)
        for p in (0, 1):
            scatters[ch].append(x_scatter(p, ch, *weights[p], pair[p]))
        cores.extend(pair)

    def scatter_down(ch):
        z_finish(1, ch)
        copy = cores_send(2, ch, *weights[2])
        if ch + 1 < CHUNKS:
            z_pass(0, ch + 1)
        x_combine(0, ch, scatters[ch][0])
        x_combine(1, ch, scatters[ch][1])
        scatters[ch].append(x_scatter(2, ch, *weights[2], copy))
        cores.append(copy)

    def gather(ch):
        gathers[ch], forwards[ch] = activate(ch, scatters[ch])

    for ch in range(CHUNKS):
        scatter_forward(ch)
        if ch > 0:
            gather(ch - 1)
        scatter_down(ch)
        if ch > 0:
            pass_on(ch - 1, gathers[ch - 1], forwards[ch - 1])
        x_combine(2, ch, scatters[ch][2])
        if ch > 0:
            pass_rest(ch - 1, gathers[ch - 1], forwards[ch - 1])
            give_back(ch - 1, forwards[ch - 1])
    last = CHUNKS - 1
    gather(last)
    for ch in range(last):
        pass_back(ch)
    pass_on(last, gathers[last], forwards[last])
    pass_rest(last, gathers[last], forwards[last])
    give_back(last, forwards[last])

    for a, grad in ((0, grad_gate), (1, grad_up)):
        for c in range(CORES):
            value = None
            for ch in range(CHUNKS):
                total = nz * PARTS[ch]
                term = mm_tn(rows[ch, :total], acts[(a * CHUNKS + ch) * CORES + c, :total])
                value = term if value is None else value + term
            grad[:, c * half : (c + 1) * half] = value.astype(BF)

    stores = []
    for source, target in ((grad_gate, grad_gate_h), (grad_up, grad_up_h)):
        stores.append(pltpu.make_async_copy(source, target, l_s.at[len(loads) + len(stores)]))
        stores[-1].start()
    y_back = {}
    for k in near_first(ny):
        t, device = at_y(k)
        y_back[k] = remote(block(yback, t, blk), block(yret, y, blk), e_ss.at[k], e_rs.at[k], device)

    for ch in range(CHUNKS):
        if ch == last:
            pass_back(ch)
        add_back(ch)
        part = PARTS[ch]
        spread = None
        for g in range(groups):
            first = g * per_z + starts[ch]
            term = mm(unpack[:, first : first + part], zsum[ch * groups + g, :part])
            spread = term if spread is None else spread + term
        spread = spread.astype(BF)
        for t in range(ch, ny, CHUNKS):
            yback[t * blk : (t + 1) * blk] = spread[t * blk : (t + 1) * blk]

        def step(parity):
            for k in near_first(ny):
                if (k + parity) % 2 == ch:
                    y_back[k].start()

        for parity in range(2):
            pl.when(y % 2 == parity)(functools.partial(step, parity))
    here = pl.ds(pl.multiple_of(y * blk, 16), blk)
    yret[here] = yback[here]
    arrived(y_back)
    in_grad_t[...] = mm_tn(yret[...], pick[...]).astype(BF)
    stores.append(pltpu.make_async_copy(in_grad_t, in_grad_h, l_s.at[len(loads) + len(stores)]))
    stores[-1].start()

    for a in range(2):
        for ch in range(CHUNKS):
            z_sent(a * CHUNKS + ch, ch)
    for copy in stores:
        copy.wait()
    for ch in range(CHUNKS):
        back_sent(ch)
    flat = [y_in, y_gr, y_back, *gathers]
    for each in scatters:
        flat.extend(each)
    for copies in flat:
        for copy in copies.values():
            copy.wait_send()
    for copy in cores:
        copy.wait_send()
    for each in forwards:
        for copy in each:
            copy.wait_send()


def per_device(sizes, out_grad, inputs, expert_ids, gate_weights, w_gate, w_up, w_down):
    nx, ny, nz = sizes
    tokens, feature = out_grad.shape
    hidden = w_gate.shape[1]
    half = hidden // CORES
    groups = nz // HSPLIT
    slots = ny * groups * SLOT
    per_z = ny * CAP
    part = max(PARTS)
    total = nz * part
    shard = total // nx
    dma = pltpu.SemaphoreType.DMA
    vmem = pltpu.VMEM
    in_grad_t, grad_gate, grad_up = pl.pallas_call(
        functools.partial(kernel, sizes),
        out_shape=(
            jax.ShapeDtypeStruct((feature, tokens), BF),
            jax.ShapeDtypeStruct((feature, hidden), BF),
            jax.ShapeDtypeStruct((feature, hidden), BF),
        ),
        in_specs=[pl.BlockSpec(memory_space=pltpu.HBM)] * 7,
        out_specs=(pl.BlockSpec(memory_space=pltpu.HBM),) * 3,
        scratch_shapes=[
            vmem((feature, tokens), BF),
            vmem((feature, hidden), BF),
            vmem((feature, hidden), BF),
            vmem((feature, tokens), BF),
            vmem((feature, tokens), BF),
            vmem((expert_ids.shape[1], tokens), jnp.int32),
            vmem((expert_ids.shape[1], tokens), F32),
            vmem((feature, hidden), BF),
            vmem((feature, hidden), BF),
            vmem((feature, hidden), BF),
            vmem((slots, tokens), BF),
            vmem((2, slots, feature), BF),
            vmem((2, slots, feature), BF),
            vmem((2 * CHUNKS * groups, part, feature), BF),
            vmem((2 * CHUNKS, total, feature), BF),
            vmem((3 * CHUNKS, total, half), BF),
            vmem((3 * CHUNKS, total, half), BF),
            vmem((3 * CHUNKS, total, half), F32),
            vmem((3 * CHUNKS, total, half), BF),
            vmem((3 * CHUNKS, 7, shard, half), BF),
            vmem((3 * CHUNKS, 2, shard, half), BF),
            vmem((2 * CHUNKS * CORES, total, half), BF),
            vmem((CHUNKS, total, feature), BF),
            vmem((CHUNKS, 8, part, feature), BF),
            vmem((CHUNKS, 3, part, feature), BF),
            vmem((CHUNKS * groups, part, feature), BF),
            vmem((slots, feature), BF),
            vmem((slots, feature), BF),
            dma((2, ny)),
            dma((2, ny)),
            dma((2 * CHUNKS, 8)),
            dma((2 * CHUNKS, nz)),
            dma((3 * CHUNKS,)),
            dma((3 * CHUNKS,)),
            dma((3 * CHUNKS, 7)),
            dma((3 * CHUNKS, 7)),
            dma((2 * CHUNKS, nx)),
            dma((2 * CHUNKS, nx)),
            dma((2 * CHUNKS, nx)),
            dma((2 * CHUNKS, nx)),
            dma((CHUNKS, 8)),
            dma((CHUNKS, 8)),
            dma((ny,)),
            dma((ny,)),
            dma((10,)),
        ],
        compiler_params=pltpu.CompilerParams(
            collective_id=0, has_side_effects=True, vmem_limit_bytes=56 * 1024 * 1024
        ),
        cost_estimate=pl.CostEstimate(
            flops=14 * nz * per_z * feature * hidden, bytes_accessed=4_000_000, transcendentals=0
        ),
    )(out_grad.T, inputs.T, expert_ids.T, gate_weights.T, w_gate, w_up, w_down.T)
    return in_grad_t.T, grad_gate, grad_up


def solution(mesh, sizes=None):
    if sizes is None:
        ny, nz = grid_of(mesh.shape["expert"])
        sizes = (mesh.shape["dp"] // CORES, ny, nz)
    placed = (
        P("expert", "dp"),
        P("expert", "dp"),
        P("expert", None),
        P("expert", None),
        P("dp", "expert"),
        P("dp", "expert"),
        P("expert", "dp"),
    )
    return jax.shard_map(
        functools.partial(per_device, sizes),
        mesh=mesh,
        in_specs=placed,
        out_specs=(P("expert", "dp"), P("dp", "expert"), P("dp", "expert")),
        check_vma=False,
    )
```
